512 devices in a mesh: dp: 64 (over x, y, z_hi, core), tensor: 8 (over z_lo).
Axes of the slice: x: 4, y: 4, z: 16 (z_hi: 2, z_lo: 8; z = z_hi * 8 + z_lo), core: 2. Of those that a mesh axis runs over, the one named last changes fastest.
Arguments:
- train_inputs: bfloat16 [32768, 5120], P('dp', 'tensor'), may hold values from -6 to 6
- train_cotangent: bfloat16 [32768, 2, 1024], P('dp', None, 'tensor'), may hold values from -0.032958984 to 0.032958984
- frozen_projection_weight: bfloat16 [2, 5120, 1024], P(None, None, 'tensor'), may hold values from -0.078125 to 0.078125
- decode_rows: bfloat16 [4096, 5120], P('dp'), may hold values from -6 to 6
- entry_master: float32 [2, 64, 5120], P(None, 'dp', 'tensor'), may hold values from -0.078125 to 0.078125
- exit_master: float32 [2, 64, 1024], P(None, 'dp', 'tensor'), may hold values from -0.36 to 0.36
- entry_moment: float32 [2, 64, 5120], P(None, 'dp', 'tensor'), may hold values from -3 to 3
- entry_square: float32 [2, 64, 5120], P(None, 'dp', 'tensor'), may hold values from 0.01 to 0.1
- exit_moment: float32 [2, 64, 1024], P(None, 'dp', 'tensor'), may hold values from -3 to 3
- exit_square: float32 [2, 64, 1024], P(None, 'dp', 'tensor'), may hold values from 0.01 to 0.1
Outputs:
- projected: bfloat16 [4096, 2, 1024], P('dp', None, 'tensor')
- entry_after: float32 [2, 64, 5120], P(None, 'dp', 'tensor')
- exit_after: float32 [2, 64, 1024], P(None, 'dp', 'tensor')
- moment_entry: float32 [2, 64, 5120], P(None, 'dp', 'tensor')
- square_entry: float32 [2, 64, 5120], P(None, 'dp', 'tensor')
- moment_exit: float32 [2, 64, 1024], P(None, 'dp', 'tensor')
- square_exit: float32 [2, 64, 1024], P(None, 'dp', 'tensor')
The draws below stay inside these ranges and needn't reach their ends.
All inputs are finite; a program needn't handle non-finite values.
Results may differ from the reference program's by a relative error of at most 0.0057.
Values may be sent and summed in bfloat16 or wider, within the bound.
A program may use at most 64 MiB of HBM per device.

```python
import math
import jax
import jax.numpy as jnp

D = 5120
KV = 1024
R = 64
TOK_DEV = 512
TOKENS = 32768
ROWS_ALL = 4096
N_DP = 64


def steps_of(stream_key, extent, cuts, low, high):
    gain, own = 1.0, jax.random.fold_in(stream_key, 6)
    for position, shards_of in cuts:
        steps = jnp.exp(jax.random.uniform(jax.random.fold_in(own, position), (shards_of,), jnp.float32, low / len(cuts), high / len(cuts)))
        gain = gain * jnp.repeat(steps, extent[position] // shards_of).reshape([-1 if axis == position else 1 for axis in range(len(extent))])
    return gain


def normal_values(rng, dims, deviation, bound, shards=(), dtype=jnp.bfloat16):
    result = deviation * jax.random.normal(rng, dims, jnp.float32)
    if shards:
        result = result * steps_of(rng, dims, shards, -0.22, 0.18)
    return jnp.clip(result, -bound, bound).astype(dtype)


def setup_inputs(seed: int = 0) -> dict:
    seeds = jax.random.split(jax.random.key(seed), 11)
    return {
        "train_inputs": normal_values(seeds[0], (TOKENS, D), 1.0, 6.0, ((0, 64), (1, 8))),
        "train_cotangent": normal_values(seeds[1], (TOKENS, 2, KV), (1.0 / (TOK_DEV * N_DP) ** 0.5), 0.032958984, ((0, 64), (2, 8))),
        "frozen_projection_weight": normal_values(seeds[2], (2, D, KV), D ** -0.5, 0.078125, ((2, 8),)),
        "decode_rows": normal_values(seeds[3], (ROWS_ALL, D), 1.0, 6.0, ((0, 64),)),
        "entry_master": normal_values(seeds[4], (2, R, D), D ** -0.5, 0.078125, ((1, 64), (2, 8)), jnp.float32),
        "exit_master": normal_values(seeds[5], (2, R, KV), 0.06, 0.36, ((1, 64), (2, 8)), jnp.float32),
        "entry_moment": normal_values(seeds[6], (2, R, D), 0.5, 3.0, ((1, 64), (2, 8)), jnp.float32),
        "entry_square": jnp.clip(jnp.exp(math.log(0.1) - 2.3025851 * jax.random.uniform(seeds[7], (2, R, D), jnp.float32) ** steps_of(seeds[7], (2, R, D), ((1, 64), (2, 8)), -0.2, 0.2)), 0.01, 0.1),
        "exit_moment": normal_values(seeds[8], (2, R, KV), 0.5, 3.0, ((1, 64), (2, 8)), jnp.float32),
        "exit_square": jnp.clip(jnp.exp(math.log(0.1) - 2.3025851 * jax.random.uniform(seeds[9], (2, R, KV), jnp.float32) ** steps_of(seeds[9], (2, R, KV), ((1, 64), (2, 8)), -0.2, 0.2)), 0.01, 0.1),
    }


adapter_scale_factor = 2.0
beta_first = 0.9
beta_second = 0.999
correct_first = 1.0 - 0.9 ** 10
correct_second = 1.0 - 0.999 ** 10
learn_rate = 0.002
decay_rate = 0.01
epsilon = 1e-08

def adam_step(master, moment, square, grad):
    moment_new = beta_first * moment + (1.0 - beta_first) * grad
    square_new = beta_second * square + (1.0 - beta_second) * grad * grad
    update = moment_new / correct_first / (jnp.sqrt(square_new / correct_second) + epsilon)
    return (master - learn_rate * (update + decay_rate * master), moment_new, square_new)

def reference(train_inputs, train_cotangent, frozen_projection_weight, decode_rows, entry_master, exit_master, entry_moment, entry_square, exit_moment, exit_square):
    entry_used = entry_master.astype(jnp.bfloat16).astype(jnp.float32)
    exit_used = exit_master.astype(jnp.bfloat16).astype(jnp.float32)
    input_full_rows = train_inputs.astype(jnp.float32)
    cotangent_full_rows = train_cotangent.astype(jnp.float32)
    reduced_product = jnp.einsum('td,prd->tpr', input_full_rows, entry_used).astype(jnp.bfloat16).astype(jnp.float32)
    backward_product = jnp.einsum('tpk,prk->tpr', cotangent_full_rows, exit_used).astype(jnp.bfloat16).astype(jnp.float32)
    down_factor_gradient = adapter_scale_factor * jnp.einsum('kje,ks->jes', backward_product, input_full_rows)
    up_factor_gradient = adapter_scale_factor * jnp.einsum('sco,scb->cob', reduced_product, cotangent_full_rows)
    entry_after, moment_entry, square_entry = adam_step(entry_master, entry_moment, entry_square, down_factor_gradient)
    exit_after, moment_exit, square_exit = adam_step(exit_master, exit_moment, exit_square, up_factor_gradient)
    down_factor_shard = entry_after.astype(jnp.bfloat16).astype(jnp.float32)
    up_factor_shard = exit_after.astype(jnp.bfloat16).astype(jnp.float32)
    combined_weight = frozen_projection_weight.astype(jnp.float32) + adapter_scale_factor * jnp.einsum('soa,soe->sae', down_factor_shard, up_factor_shard)
    combined_weight = combined_weight.astype(jnp.bfloat16).astype(jnp.float32)
    projected = jnp.einsum('nd,pdk->npk', decode_rows.astype(jnp.float32), combined_weight).astype(jnp.bfloat16)
    return (projected, entry_after, exit_after, moment_entry, square_entry, moment_exit, square_exit)
```

```python
import functools

import jax
import jax.numpy as jnp
from jax import lax
from jax.experimental import pallas as pl
from jax.experimental.pallas import tpu as pltpu
from jax.sharding import PartitionSpec as P

adapter_scale_factor = 2.0
beta_first = 0.9
beta_second = 0.999
correct_first = 1.0 - 0.9**10
correct_second = 1.0 - 0.999**10
learn_rate = 0.002
decay_rate = 0.01
epsilon = 1e-08

BF = jnp.bfloat16
F32 = jnp.float32
QUAD = 4


def adam_step(master, moment, square, grad):
    moment_new = beta_first * moment + (1.0 - beta_first) * grad
    square_new = beta_second * square + (1.0 - beta_second) * grad * grad
    update = moment_new / correct_first / (jnp.sqrt(square_new / correct_second) + epsilon)
    return (master - learn_rate * (update + decay_rate * master), moment_new, square_new)


def dot(a, b, ca, cb):
    return lax.dot_general(a, b, (((ca,), (cb,)), ((), ())), preferred_element_type=F32)


def kernel(
    nx, ny, nt,
    x_hbm, cot_hbm, frz_hbm, dec_hbm, em_hbm, xm_hbm, emo_hbm, esq_hbm, xmo_hbm, xsq_hbm,
    proj_o, new_o,
    em, xm, emo, xmo, esq, xsq, x_v, cot_v, frz_v, dec_v, cotd, wide, base,
    pack, rp, qa, ea, qb, eb, fac, exf, lbf, lbs, lt, lfull,
    gr, r1, rs, r2, zs, z1, zf,
    local_sem, send_sem, recv_sem,
):
    planes = nx * ny
    rank = planes * QUAD
    me = lax.axis_index("dp")
    t = lax.axis_index("tensor")
    xy = lax.div(me, QUAD)
    q = lax.rem(me, QUAD)
    xi, yi = lax.div(xy, ny), lax.rem(xy, ny)
    zh, co = lax.div(q, 2), lax.rem(q, 2)

    def plane_peer(k):
        return lax.rem(xi + k // ny, nx) * ny + lax.rem(yi + k % ny, ny)

    def quad_peer(m):
        return lax.rem(zh + m // 2, 2) * 2 + lax.rem(co + m % 2, 2)

    plane = [(k, plane_peer(k)) for k in range(1, planes)]
    quad = [(m, quad_peer(m)) for m in (3, 2, 1)]
    tens = [(k, lax.rem(t + k, nt)) for k in range(1, nt)]

    def send(stage, src, dst, dp, tn):
        pltpu.make_async_remote_copy(
            src_ref=src, dst_ref=dst, send_sem=send_sem.at[stage], recv_sem=recv_sem.at[stage],
            device_id=(dp, tn), device_id_type=pl.DeviceIdType.MESH,
        ).start()

    def descriptor(stage, ref):
        return pltpu.make_async_remote_copy(
            src_ref=ref, dst_ref=ref, send_sem=send_sem.at[stage], recv_sem=recv_sem.at[stage],
            device_id=(me, lax.rem(t + 1, nt)), device_id_type=pl.DeviceIdType.MESH,
        )

    loads = [
        pltpu.make_async_copy(src, dst, local_sem.at[i])
        for i, (src, dst) in enumerate(
            (
                (em_hbm, em),
                (xm_hbm, xm),
                (emo_hbm, emo),
                (xmo_hbm, xmo),
                (esq_hbm, esq),
                (xsq_hbm, xsq),
                (cot_hbm, cot_v),
                (x_hbm, x_v),
                (dec_hbm, dec_v),
                (frz_hbm, frz_v),
            )
        )
    ]
    for load in loads:
        load.start()

    barrier = pltpu.get_barrier_semaphore()
    peers = (
        [(pp * QUAD + q, t) for _, pp in plane]
        + [(xy * QUAD + qq, t) for _, qq in quad]
        + [(me, tt) for _, tt in tens]
    )
    for peer in peers:
        pl.semaphore_signal(barrier, inc=1, device_id=peer, device_id_type=pl.DeviceIdType.MESH)

    pack[...] = jnp.zeros_like(pack)
    for i, (e_ref, o_ref) in enumerate(((em, xm), (emo, xmo), (esq, xsq))):
        loads[2 * i].wait()
        loads[2 * i + 1].wait()
        for p in range(2):
            for c in range(5):
                pack[i, p * 6 + c : p * 6 + c + 1, :] = e_ref[p, :, c * 128 : (c + 1) * 128]
            pack[i, p * 6 + 5 : p * 6 + 6, :] = o_ref[p, :, :]
    qa[q] = pack[0].astype(BF)
    exf[...] = jnp.zeros_like(exf)
    rs[...] = jnp.zeros_like(rs)

    pl.semaphore_wait(barrier, len(peers))

    def gather_rows(stage, slots, rows):
        for _, qq in quad:
            send(stage, slots.at[q], slots.at[q], xy * QUAD + qq, t)
        yield
        descriptor(stage, slots.at[pl.ds(0, 3)]).wait_recv()
        four = slots[...].astype(F32)
        for j in range(QUAD):
            rp[j * 12 : (j + 1) * 12, :] = four[j, :12, :]
        rows[xy] = rp[...].astype(BF)
        for _, pp in plane:
            send(stage + 1, rows.at[xy], rows.at[xy], pp * QUAD + q, t)
        yield
        descriptor(stage + 1, rows.at[pl.ds(0, planes - 1)]).wait_recv()
        wide[0 : rank * 12, :] = rows[...].reshape(rank * 12, 128).astype(F32)
        for p in range(2):
            here = slice(p * rank, (p + 1) * rank)
            for c in range(5):
                fac[here, c * 128 : (c + 1) * 128] = wide[
                    pl.ds(p * 6 + c, rank, stride=12), :
                ].astype(BF)
            exf[here, p * 128 : (p + 1) * 128] = wide[pl.ds(p * 6 + 5, rank, stride=12), :].astype(BF)
        yield

    first = gather_rows(0, qa, ea)
    next(first)
    loads[6].wait()
    tokens = x_v.shape[0]
    wide[0 : 2 * tokens, :] = cot_v[...].astype(F32)
    for p in range(2):
        cotd[:, p * 128 : (p + 1) * 128] = wide[pl.ds(p, tokens, stride=2), :].astype(BF)
    next(first)
    loads[7].wait()
    next(first)

    lbf[:, : 2 * rank] = dot(x_v[...], fac[...], 1, 1)
    lbf[:, 2 * rank :] = dot(cotd[...], exf[...], 1, 1)
    lbs[...] = lbf[...].astype(BF).reshape(lbs.shape)
    for k, tt in tens[::-1]:
        send(2, lbs.at[tt], lt.at[k - 1], me, tt)
    loads[8].wait()
    loads[9].wait()
    for p in range(2):
        base[:, p * 128 : (p + 1) * 128] = dot(dec_v[...], frz_v[p], 1, 0)
    part = tokens // nt
    descriptor(2, lt).wait_recv()
    total = lbf[pl.ds(pl.multiple_of(t * part, part), part), :]
    for k in range(nt - 1):
        total = total + lt[k].astype(F32)
    lfull[t] = total.astype(BF)
    for k, tt in tens[::-1]:
        send(3, lfull.at[t], lfull.at[t], me, tt)
    descriptor(3, lfull.at[pl.ds(0, nt - 1)]).wait_recv()

    low = lfull[:, :, : 2 * rank].reshape(tokens, 2 * rank)
    back = lfull[:, :, 2 * rank :].reshape(tokens, 2 * rank)
    g_in = adapter_scale_factor * dot(back, x_v[...], 0, 0)
    g_out = adapter_scale_factor * dot(low, cotd[...], 0, 0)
    for p in range(2):
        here = slice(p * rank, (p + 1) * rank)
        for c in range(5):
            gr[pl.ds(p * 6 + c, rank, stride=12), :] = g_in[here, c * 128 : (c + 1) * 128]
        gr[pl.ds(p * 6 + 5, rank, stride=12), :] = g_out[here, p * 128 : (p + 1) * 128]
    for k, pp in plane:
        send(4, gr.at[pl.ds(pl.multiple_of(pp * 48, 48), 48)], r1.at[k - 1], pp * QUAD + q, t)
    descriptor(4, r1).wait_recv()
    total = gr[pl.ds(pl.multiple_of(xy * 48, 48), 48), :]
    for k in range(planes - 1):
        total = total + r1[k]
    for j in range(QUAD):
        rs[j, :12, :] = total[j * 12 : (j + 1) * 12, :]
    for m, qq in quad:
        send(5, rs.at[qq], r2.at[m - 1], xy * QUAD + qq, t)
    descriptor(5, r2).wait_recv()
    grad = rs[q] + r2[0] + r2[1] + r2[2]

    after, moment, square = adam_step(pack[0], pack[1], pack[2], grad)
    qb[q] = after.astype(BF)
    second = gather_rows(6, qb, eb)
    next(second)
    for i, value in enumerate((after, moment, square)):
        new_o[i] = value
    next(second)
    next(second)

    feats = x_v.shape[1]
    mine = dec_v[:, pl.ds(pl.multiple_of(t * feats, feats), feats)]
    zs[...] = dot(mine, fac[...], 1, 1)
    for k, tt in tens[::-1]:
        send(8, zs.at[pl.ds(pl.multiple_of(tt * 8, 8), 8)], z1.at[k - 1], me, tt)
    descriptor(8, z1).wait_recv()
    total = zs[pl.ds(pl.multiple_of(t * 8, 8), 8), :]
    for k in range(nt - 1):
        total = total + z1[k]
    zf[t] = total
    for k, tt in tens[::-1]:
        send(9, zf.at[t], zf.at[t], me, tt)
    descriptor(9, zf.at[pl.ds(0, nt - 1)]).wait_recv()
    inner = (adapter_scale_factor * zf[...]).reshape(8 * nt, 2 * rank).astype(BF)
    out = base[...] + dot(inner, exf[...], 1, 0)
    for p in range(2):
        wide[pl.ds(p, 8 * nt, stride=2), :] = out[:, p * 128 : (p + 1) * 128]
    proj_o[...] = wide[0 : 16 * nt, :].astype(BF)

    for stage, ref in (
        (0, qa.at[pl.ds(0, 3)]),
        (1, ea.at[pl.ds(0, planes - 1)]),
        (2, lt),
        (3, lfull.at[pl.ds(0, nt - 1)]),
        (4, r1),
        (5, r2),
        (6, qb.at[pl.ds(0, 3)]),
        (7, eb.at[pl.ds(0, planes - 1)]),
        (8, z1),
        (9, zf.at[pl.ds(0, nt - 1)]),
    ):
        descriptor(stage, ref).wait_send()


def spread(new, proj, *rest):
    outs, parts, sem = rest[:7], rest[7:13], rest[13]
    copies = [pltpu.make_async_copy(proj, outs[0], sem.at[0])]
    copies[0].start()
    for i, (e, o) in enumerate(((0, 1), (2, 4), (3, 5))):
        for p in range(2):
            for c in range(5):
                row = p * 6 + c
                parts[e][p, :, c * 128 : (c + 1) * 128] = new[i, row : row + 1, :]
            parts[o][p, :, :] = new[i, p * 6 + 5 : p * 6 + 6, :]
        for n in (e, o):
            copies.append(pltpu.make_async_copy(parts[n], outs[n + 1], sem.at[n + 1]))
            copies[-1].start()
    for copy in copies:
        copy.wait()


def body(nx, ny, nt, x, cot, frz, dec, em, xm, emo, esq, xmo, xsq):
    tokens, feats = x.shape
    rows = dec.shape[0]
    planes = nx * ny
    rank = planes * QUAD
    part = tokens // nt
    hbm = pl.BlockSpec(memory_space=pltpu.HBM)
    vmem = pl.BlockSpec(memory_space=pltpu.VMEM)
    like = lambda a: jax.ShapeDtypeStruct(a.shape, a.dtype)
    held = lambda a: pltpu.VMEM(a.shape, a.dtype)
    proj, new = pl.pallas_call(
        functools.partial(kernel, nx, ny, nt),
        out_shape=(
            jax.ShapeDtypeStruct((rows * 2, 128), BF),
            jax.ShapeDtypeStruct((3, 16, 128), F32),
        ),
        in_specs=[hbm] * 10,
        out_specs=[vmem] * 2,
        scratch_shapes=[
            held(em), held(xm), held(em), held(xm), held(em), held(xm),
            held(x),
            pltpu.VMEM((tokens * 2, 128), BF),
            held(frz),
            held(dec),
            pltpu.VMEM((tokens, 256), BF),
            pltpu.VMEM((max(2 * tokens, rank * 12), 128), F32),
            pltpu.VMEM((rows, 256), F32),
            pltpu.VMEM((3, 16, 128), F32),
            pltpu.VMEM((48, 128), F32),
            pltpu.VMEM((QUAD, 16, 128), BF),
            pltpu.VMEM((planes, 48, 128), BF),
            pltpu.VMEM((QUAD, 16, 128), BF),
            pltpu.VMEM((planes, 48, 128), BF),
            pltpu.VMEM((2 * rank, feats), BF),
            pltpu.VMEM((2 * rank, 256), BF),
            pltpu.VMEM((tokens, 4 * rank), F32),
            pltpu.VMEM((nt, part, 4 * rank), BF),
            pltpu.VMEM((nt - 1, part, 4 * rank), BF),
            pltpu.VMEM((nt, part, 4 * rank), BF),
            pltpu.VMEM((rank * 12, 128), F32),
            pltpu.VMEM((planes - 1, 48, 128), F32),
            pltpu.VMEM((QUAD, 16, 128), F32),
            pltpu.VMEM((3, 16, 128), F32),
            pltpu.VMEM((rows, 2 * rank), F32),
            pltpu.VMEM((nt - 1, 8, 2 * rank), F32),
            pltpu.VMEM((nt, 8, 2 * rank), F32),
            pltpu.SemaphoreType.DMA((10,)),
            pltpu.SemaphoreType.DMA((10,)),
            pltpu.SemaphoreType.DMA((10,)),
        ],
        compiler_params=pltpu.CompilerParams(
            collective_id=0, has_side_effects=True, vmem_limit_bytes=63 * 1024 * 1024
        ),
        cost_estimate=pl.CostEstimate(flops=600_000_000, bytes_accessed=5_000_000, transcendentals=0),
    )(x, cot.reshape(tokens * 2, 128), frz, dec, em, xm, emo, esq, xmo, xsq)
    factors = [em, xm, em, em, xm, xm]
    out = pl.pallas_call(
        spread,
        out_shape=(like(proj),) + tuple(like(f) for f in factors),
        in_specs=[vmem] * 2,
        out_specs=[hbm] * 7,
        scratch_shapes=[held(f) for f in factors] + [pltpu.SemaphoreType.DMA((7,))],
        cost_estimate=pl.CostEstimate(flops=10_000, bytes_accessed=60_000, transcendentals=0),
    )(new, proj)
    return (out[0].reshape(rows, 2, 128),) + tuple(out[1:])


def solution(mesh):
    nt = mesh.shape["tensor"]
    side = 4 if mesh.shape["dp"] == 64 else 2
    ny = side
    nx = mesh.shape["dp"] // (QUAD * ny)
    factor = P(None, "dp", "tensor")
    return jax.shard_map(
        functools.partial(body, nx, ny, nt),
        mesh=mesh,
        in_specs=(
            P("dp", "tensor"),
            P("dp", None, "tensor"),
            P(None, None, "tensor"),
            P("dp", None),
        )
        + (factor,) * 6,
        out_specs=(P("dp", None, "tensor"),) + (factor,) * 6,
        check_vma=False,
    )
```

```python
import functools

import jax
import jax.numpy as jnp
from jax import lax
from jax.experimental import pallas as pl
from jax.experimental.pallas import tpu as pltpu
from jax.sharding import PartitionSpec as P

adapter_scale_factor = 2.0
beta_first = 0.9
beta_second = 0.999
correct_first = 1.0 - 0.9**10
correct_second = 1.0 - 0.999**10
learn_rate = 0.002
decay_rate = 0.01
epsilon = 1e-08

BF = jnp.bfloat16
F32 = jnp.float32
QUAD = 4


def adam_step(master, moment, square, grad):
    moment_new = beta_first * moment + (1.0 - beta_first) * grad
    square_new = beta_second * square + (1.0 - beta_second) * grad * grad
    update = moment_new / correct_first / (jnp.sqrt(square_new / correct_second) + epsilon)
    return (master - learn_rate * (update + decay_rate * master), moment_new, square_new)


def dot(a, b, ca, cb):
    return lax.dot_general(a, b, (((ca,), (cb,)), ((), ())), preferred_element_type=F32)


def kernel(
    nx, ny, nt,
    x_hbm, cot_hbm, frz_hbm, dec_hbm, em_hbm, xm_hbm, emo_hbm, esq_hbm, xmo_hbm, xsq_hbm,
    proj_o, new_o,
    em, xm, emo, xmo, esq, xsq, xc, cot_v, frz_v, dec_v, dec2, wide, base,
    pack, ga, gb, fac, enew, xnew, lbf, lbs, l1, l2s, l2, lfull,
    gr, r1, rs, r2, zs, zl, zx,
    local_sem, send_sem, recv_sem,
):
    planes = nx * ny
    group = planes * 2
    quads = nt // 2
    tokens = xc.shape[0]
    feats = em_hbm.shape[2]
    me = lax.axis_index("dp")
    t = lax.axis_index("tensor")
    xy = lax.div(me, QUAD)
    q = lax.rem(me, QUAD)
    xi, yi = lax.div(xy, ny), lax.rem(xy, ny)
    zh, co = lax.div(q, 2), lax.rem(q, 2)
    tq, ti = lax.div(t, quads), lax.rem(t, quads)
    s = xy * 2 + co

    def plane_peer(k):
        return lax.rem(xi + k // ny, nx) * ny + lax.rem(yi + k % ny, ny)

    def device(pp, z, c):
        return pp * QUAD + z * 2 + c

    other_zh, other_co = 1 - zh, 1 - co
    order = sorted(
        range(1, planes), key=lambda k: -(min(k // ny, nx - k // ny) + min(k % ny, ny - k % ny))
    )
    plane = [(k, plane_peer(k)) for k in order]
    near = [device(pp, zh, c) for _, pp in plane for c in (co, other_co)]
    near.append(device(xy, zh, other_co))
    partner = device(xy, other_zh, co)
    cross = device(xy, other_zh, other_co)
    ring = sorted(range(1, nt), key=lambda k: abs(k - nt // 2))
    tens = [(k, lax.rem(t + k, nt)) for k in ring]
    quad = [(k, tq * quads + lax.rem(ti + k, quads)) for k in range(1, quads)]
    opposite = (1 - tq) * quads + ti

    def send(stage, src, dst, dp, tn):
        pltpu.make_async_remote_copy(
            src_ref=src, dst_ref=dst, send_sem=send_sem.at[stage], recv_sem=recv_sem.at[stage],
            device_id=(dp, tn), device_id_type=pl.DeviceIdType.MESH,
        ).start()

    def descriptor(stage, ref):
        return pltpu.make_async_remote_copy(
            src_ref=ref, dst_ref=ref, send_sem=send_sem.at[stage], recv_sem=recv_sem.at[stage],
            device_id=(partner, t), device_id_type=pl.DeviceIdType.MESH,
        )

    sent = []

    def arrive(stage, ref):
        descriptor(stage, ref).wait_recv()
        sent.append((stage, ref))

    barrier = pltpu.get_barrier_semaphore()
    peers = [(partner, t), (cross, t)] + [(dp, t) for dp in near]
    peers += [(dp, tt) for _, tt in tens for dp in (me, partner)]
    for peer in peers:
        pl.semaphore_signal(barrier, inc=1, device_id=peer, device_id_type=pl.DeviceIdType.MESH)

    here = pl.ds(pl.multiple_of(t * feats, feats), feats)
    loads = [
        pltpu.make_async_copy(src, dst, local_sem.at[i])
        for i, (src, dst) in enumerate(
            (
                (em_hbm, em),
                (xm_hbm, xm),
                (emo_hbm, emo),
                (xmo_hbm, xmo),
                (esq_hbm, esq),
                (xsq_hbm, xsq),
                (cot_hbm, cot_v),
                (x_hbm, xc.at[:, pl.ds(0, feats)]),
                (dec_hbm.at[:, here], dec2.at[0]),
                (dec_hbm, dec_v),
                (frz_hbm, frz_v),
            )
        )
    ]
    for load in loads:
        load.start()

    pack[...] = jnp.zeros_like(pack)
    for i, (e_ref, o_ref) in enumerate(((em, xm), (emo, xmo), (esq, xsq))):
        loads[2 * i].wait()
        loads[2 * i + 1].wait()
        for p in range(2):
            for c in range(5):
                pack[i, p * 6 + c : p * 6 + c + 1, :] = e_ref[p, :, c * 128 : (c + 1) * 128]
            pack[i, p * 6 + 5 : p * 6 + 6, :] = o_ref[p, :, :]
    ga[0, s] = pack[0].astype(BF)
    fac[...] = jnp.zeros_like(fac)
    xnew[...] = jnp.zeros_like(xnew)
    rs[...] = jnp.zeros_like(rs)
    loads[6].wait()
    wide[0 : 2 * tokens, :] = cot_v[...].astype(F32)
    for p in range(2):
        xc[:, feats + p * 128 : feats + (p + 1) * 128] = wide[pl.ds(p, tokens, stride=2), :].astype(BF)
    loads[7].wait()
    loads[8].wait()

    pl.semaphore_wait(barrier, len(peers))

    def spread_rows(stage, rows, half):
        for dp in near:
            send(stage, rows.at[half, s], rows.at[half, s], dp, t)

    all_rows = lambda rows, half: rows.at[half, pl.ds(0, group - 1)]
    send(1, ga.at[0, s], ga.at[1, s], partner, t)
    spread_rows(0, ga, 0)
    send(18, dec2.at[0], dec2.at[1], partner, t)

    def unpack(rows, half, pieces, put_in, put_out):
        wide[0 : group * 16, :] = rows[half].reshape(group * 16, 128).astype(F32)
        for p in range(2):
            for c in pieces:
                piece = wide[pl.ds(p * 6 + c, group, stride=16), :].astype(BF)
                if c < 5:
                    put_in[p * group : (p + 1) * group, c * 128 : (c + 1) * 128] = piece
                else:
                    put_out(p, piece)

    def project(half):
        def put_out(p, piece):
            fac[
                half,
                (2 + p) * group : (3 + p) * group,
                feats + p * 128 : feats + (p + 1) * 128,
            ] = piece

        unpack(ga, half, range(6), fac.at[half], put_out)
        lbf[half] = dot(xc[...], fac[half], 1, 1)
        lbs[half] = lbf[half].astype(BF).reshape(lbs.shape[1:])
        for k, tt in quad:
            send(3 + half, lbs.at[half, lax.rem(tt, quads)], l1.at[half, k - 1], me, tt)

    part = tokens // quads

    def sum_quad(half):
        if quads > 1:
            arrive(3 + half, l1.at[half])
        total = lbf[half, pl.ds(pl.multiple_of(ti * part, part), part), :]
        for k in range(quads - 1):
            total = total + l1[half, k].astype(F32)
        lbf[half, 0:part, :] = total
        l2s[half] = total.astype(BF)
        send(5 + half, l2s.at[half], l2.at[half], me, opposite)

    def sum_all(half):
        arrive(5 + half, l2.at[half])
        lfull[half, ti] = (lbf[half, 0:part, :] + l2[half].astype(F32)).astype(BF)
        for k, tt in quad:
            send(7 + half, lfull.at[half, ti], lfull.at[half, ti], me, tt)

    def gradients(half):
        if quads > 1:
            arrive(7 + half, lfull.at[half, pl.ds(0, quads - 1)])
        both = lfull[half].reshape(tokens, 4 * group)
        g = adapter_scale_factor * dot(both, xc[...], 0, 0)
        for p in range(2):
            for c in range(5):
                gr[half, pl.ds(p * 6 + c, group, stride=12), :] = g[
                    (2 + p) * group : (3 + p) * group, c * 128 : (c + 1) * 128
                ]
            gr[half, pl.ds(p * 6 + 5, group, stride=12), :] = g[
                p * group : (p + 1) * group, feats + p * 128 : feats + (p + 1) * 128
            ]
        for k, pp in plane:
            src = gr.at[half, pl.ds(pl.multiple_of(pp * 24, 24), 24)]
            send(9 + half, src, r1.at[half, k - 1], device(pp, zh, co), t)

    def sum_plane(half):
        if planes > 1:
            arrive(9 + half, r1.at[half])
        total = gr[half, pl.ds(pl.multiple_of(xy * 24, 24), 24), :]
        for k in range(planes - 1):
            total = total + r1[half, k]
        for c in range(2):
            rs[half, c, :12, :] = total[c * 12 : (c + 1) * 12, :]

    arrive(0, all_rows(ga, 0))
    project(0)
    arrive(1, ga.at[1, s])
    spread_rows(2, ga, 1)
    sum_quad(0)
    arrive(2, all_rows(ga, 1))
    project(1)
    sum_all(0)
    sum_quad(1)
    gradients(0)
    sum_all(1)
    gradients(1)
    sum_plane(0)
    send(11, rs.at[0, other_co], r2.at[0], device(xy, zh, other_co), t)
    sum_plane(1)
    send(12, rs.at[1, co], r2.at[1], partner, t)
    send(12, rs.at[1, other_co], r2.at[2], cross, t)

    loads[9].wait()
    loads[10].wait()
    for p in range(2):
        base[:, p * 128 : (p + 1) * 128] = dot(dec_v[...], frz_v[p], 1, 0)

    arrive(11, r2.at[0])
    arrive(12, r2.at[pl.ds(1, 2)])
    grad = rs[0, co] + r2[0] + (r2[1] + r2[2])
    after, moment, square = adam_step(pack[0], pack[1], pack[2], grad)
    gb[0, s] = after.astype(BF)
    send(14, gb.at[0, s], gb.at[1, s], partner, t)
    spread_rows(13, gb, 0)
    for i, value in enumerate((after, moment, square)):
        new_o[i] = value
    arrive(18, dec2.at[1])
    arrive(13, all_rows(gb, 0))

    def put_new(half):
        def put_out(p, piece):
            first = (half * 2 + p) * group
            xnew[first : first + group, p * 128 : (p + 1) * 128] = piece

        return put_out

    unpack(gb, 0, range(5), enew, None)
    half_rows = dec_v.shape[0] // 2
    inner = [adapter_scale_factor * dot(dec2[i], enew[...], 1, 1) for i in range(2)]
    inner = [jnp.concatenate([v[:half_rows], v[half_rows:]], axis=1) for v in inner]
    for i in range(2):
        zs[i] = inner[i].astype(BF)
    for k, tt in tens:
        send(16, zs.at[0], zl.at[k - 1], me, tt)
    for k in range(nt):
        send(17, zs.at[1], zx.at[k], partner, lax.rem(t + k, nt))
    arrive(14, gb.at[1, s])
    spread_rows(15, gb, 1)
    unpack(gb, 0, (5,), None, put_new(0))
    arrive(15, all_rows(gb, 1))
    unpack(gb, 1, (5,), None, put_new(1))
    arrive(16, zl)
    arrive(17, zx)
    mine, theirs = inner[0], zx[0].astype(F32)
    for k in range(nt - 1):
        mine = mine + zl[k].astype(F32)
        theirs = theirs + zx[k + 1].astype(F32)
    both = jnp.concatenate(
        [
            jnp.concatenate([v[:, : 2 * group], v[:, 2 * group :]], axis=0)
            for v in (mine.astype(BF), theirs.astype(BF))
        ],
        axis=1,
    )
    out = base[...] + dot(both, xnew[...], 1, 0)
    rows = 2 * half_rows
    for p in range(2):
        wide[pl.ds(p, rows, stride=2), :] = out[:, p * 128 : (p + 1) * 128]
    proj_o[...] = wide[0 : 2 * rows, :].astype(BF)

    for stage, ref in sent:
        descriptor(stage, ref).wait_send()


def spread(new, proj, *rest):
    outs, parts, sem = rest[:7], rest[7:13], rest[13]
    copies = [pltpu.make_async_copy(proj, outs[0], sem.at[0])]
    copies[0].start()
    for i, (e, o) in enumerate(((0, 1), (2, 4), (3, 5))):
        for p in range(2):
            for c in range(5):
                row = p * 6 + c
                parts[e][p, :, c * 128 : (c + 1) * 128] = new[i, row : row + 1, :]
            parts[o][p, :, :] = new[i, p * 6 + 5 : p * 6 + 6, :]
        for n in (e, o):
            copies.append(pltpu.make_async_copy(parts[n], outs[n + 1], sem.at[n + 1]))
            copies[-1].start()
    for copy in copies:
        copy.wait()


def body(nx, ny, nt, x, cot, frz, dec, em, xm, emo, esq, xmo, xsq):
    tokens, feats = x.shape
    rows = dec.shape[0]
    planes = nx * ny
    group = planes * 2
    quads = nt // 2
    part = tokens // quads
    hbm = pl.BlockSpec(memory_space=pltpu.HBM)
    vmem = pl.BlockSpec(memory_space=pltpu.VMEM)
    like = lambda a: jax.ShapeDtypeStruct(a.shape, a.dtype)
    held = lambda a: pltpu.VMEM(a.shape, a.dtype)
    proj, new = pl.pallas_call(
        functools.partial(kernel, nx, ny, nt),
        out_shape=(
            jax.ShapeDtypeStruct((rows * 2, 128), BF),
            jax.ShapeDtypeStruct((3, 16, 128), F32),
        ),
        in_specs=[hbm] * 10,
        out_specs=[vmem] * 2,
        scratch_shapes=[
            held(em), held(xm), held(em), held(xm), held(em), held(xm),
            pltpu.VMEM((tokens, feats + 256), BF),
            pltpu.VMEM((tokens * 2, 128), BF),
            held(frz),
            held(dec),
            pltpu.VMEM((2, rows, feats), BF),
            pltpu.VMEM((max(2 * tokens, group * 16), 128), F32),
            pltpu.VMEM((rows, 256), F32),
            pltpu.VMEM((3, 16, 128), F32),
            pltpu.VMEM((2, group, 16, 128), BF),
            pltpu.VMEM((2, group, 16, 128), BF),
            pltpu.VMEM((2, 4 * group, feats + 256), BF),
            pltpu.VMEM((2 * group, feats), BF),
            pltpu.VMEM((4 * group, 256), BF),
            pltpu.VMEM((2, tokens, 4 * group), F32),
            pltpu.VMEM((2, quads, part, 4 * group), BF),
            pltpu.VMEM((2, max(quads - 1, 1), part, 4 * group), BF),
            pltpu.VMEM((2, part, 4 * group), BF),
            pltpu.VMEM((2, part, 4 * group), BF),
            pltpu.VMEM((2, quads, part, 4 * group), BF),
            pltpu.VMEM((2, group * 12, 128), F32),
            pltpu.VMEM((2, max(planes - 1, 1), 24, 128), F32),
            pltpu.VMEM((2, 2, 16, 128), F32),
            pltpu.VMEM((3, 16, 128), F32),
            pltpu.VMEM((2, rows // 2, 4 * group), BF),
            pltpu.VMEM((nt - 1, rows // 2, 4 * group), BF),
            pltpu.VMEM((nt, rows // 2, 4 * group), BF),
            pltpu.SemaphoreType.DMA((11,)),
            pltpu.SemaphoreType.DMA((19,)),
            pltpu.SemaphoreType.DMA((19,)),
        ],
        compiler_params=pltpu.CompilerParams(
            collective_id=0, has_side_effects=True, vmem_limit_bytes=63 * 1024 * 1024
        ),
        cost_estimate=pl.CostEstimate(flops=600_000_000, bytes_accessed=5_000_000, transcendentals=0),
    )(x, cot.reshape(tokens * 2, 128), frz, dec, em, xm, emo, esq, xmo, xsq)
    factors = [em, xm, em, em, xm, xm]
    out = pl.pallas_call(
        spread,
        out_shape=(like(proj),) + tuple(like(f) for f in factors),
        in_specs=[vmem] * 2,
        out_specs=[hbm] * 7,
        scratch_shapes=[held(f) for f in factors] + [pltpu.SemaphoreType.DMA((7,))],
        cost_estimate=pl.CostEstimate(flops=10_000, bytes_accessed=60_000, transcendentals=0),
    )(new, proj)
    return (out[0].reshape(rows, 2, 128),) + tuple(out[1:])


def solution(mesh):
    nt = mesh.shape["tensor"]
    planes = mesh.shape["dp"] // QUAD
    ny = min(planes, 4)
    nx = planes // ny
    factor = P(None, "dp", "tensor")
    return jax.shard_map(
        functools.partial(body, nx, ny, nt),
        mesh=mesh,
        in_specs=(
            P("dp", "tensor"),
            P("dp", None, "tensor"),
            P(None, None, "tensor"),
            P("dp", None),
        )
        + (factor,) * 6,
        out_specs=(P("dp", None, "tensor"),) + (factor,) * 6,
        check_vma=False,
    )
```

```python
import functools

import jax
import jax.numpy as jnp
from jax import lax
from jax.experimental import pallas as pl
from jax.experimental.pallas import tpu as pltpu
from jax.sharding import PartitionSpec as P

adapter_scale_factor = 2.0
beta_first = 0.9
beta_second = 0.999
correct_first = 1.0 - 0.9**10
correct_second = 1.0 - 0.999**10
learn_rate = 0.002
decay_rate = 0.01
epsilon = 1e-08

BF = jnp.bfloat16
F32 = jnp.float32
QUAD = 4


def adam_step(master, moment, square, grad):
    moment_new = beta_first * moment + (1.0 - beta_first) * grad
    square_new = beta_second * square + (1.0 - beta_second) * grad * grad
    update = moment_new / correct_first / (jnp.sqrt(square_new / correct_second) + epsilon)
    return (master - learn_rate * (update + decay_rate * master), moment_new, square_new)


def dot(a, b, ca, cb):
    return lax.dot_general(a, b, (((ca,), (cb,)), ((), ())), preferred_element_type=F32)


def kernel(
    nx, ny, nt,
    x_hbm, cot_hbm, frz_hbm, dec_hbm, em_hbm, xm_hbm, emo_hbm, esq_hbm, xmo_hbm, xsq_hbm,
    proj_o, new_o,
    em, xm, emo, xmo, esq, xsq, xc, cot_v, frz_v, dec_v, dec2, wide, base,
    pack, ga, gb, fac, enew, xnew, lbf, lbs, l1, l2s, l2, lfull,
    gr, r1, rs, r2, zs, zl,
    local_sem, send_sem, recv_sem,
):
    planes = nx * ny
    group = planes * 2
    quads = nt // 2
    tokens = xc.shape[0]
    feats = em_hbm.shape[2]
    me = lax.axis_index("dp")
    t = lax.axis_index("tensor")
    xy = lax.div(me, QUAD)
    q = lax.rem(me, QUAD)
    xi, yi = lax.div(xy, ny), lax.rem(xy, ny)
    zh, co = lax.div(q, 2), lax.rem(q, 2)
    tq, ti = lax.div(t, quads), lax.rem(t, quads)
    s = xy * 2 + co

    def plane_peer(k):
        return lax.rem(xi + k // ny, nx) * ny + lax.rem(yi + k % ny, ny)

    def device(pp, z, c):
        return pp * QUAD + z * 2 + c

    other_zh, other_co = 1 - zh, 1 - co
    order = sorted(
        range(1, planes), key=lambda k: -(min(k // ny, nx - k // ny) + min(k % ny, ny - k % ny))
    )
    plane = [(k, plane_peer(k)) for k in order]
    near = [device(pp, zh, c) for _, pp in plane for c in (co, other_co)]
    near.append(device(xy, zh, other_co))
    partner = device(xy, other_zh, co)
    cross = device(xy, other_zh, other_co)
    ring = sorted(range(1, nt), key=lambda k: abs(k - nt // 2))
    tens = [(k, lax.rem(t + k, nt)) for k in ring]
    quad = [(k, tq * quads + lax.rem(ti + k, quads)) for k in range(1, quads)]
    opposite = (1 - tq) * quads + ti

    def send(stage, src, dst, dp, tn):
        pltpu.make_async_remote_copy(
            src_ref=src, dst_ref=dst, send_sem=send_sem.at[stage], recv_sem=recv_sem.at[stage],
            device_id=(dp, tn), device_id_type=pl.DeviceIdType.MESH,
        ).start()

    def descriptor(stage, ref):
        return pltpu.make_async_remote_copy(
            src_ref=ref, dst_ref=ref, send_sem=send_sem.at[stage], recv_sem=recv_sem.at[stage],
            device_id=(partner, t), device_id_type=pl.DeviceIdType.MESH,
        )

    sent = []

    def arrive(stage, ref):
        descriptor(stage, ref).wait_recv()
        sent.append((stage, ref))

    barrier = pltpu.get_barrier_semaphore()
    peers = [(partner, t), (cross, t)] + [(dp, t) for dp in near]
    peers += [(me, tt) for _, tt in tens]
    for peer in peers:
        pl.semaphore_signal(barrier, inc=1, device_id=peer, device_id_type=pl.DeviceIdType.MESH)

    here = pl.ds(pl.multiple_of(t * feats, feats), feats)
    loads = [
        pltpu.make_async_copy(src, dst, local_sem.at[i])
        for i, (src, dst) in enumerate(
            (
                (em_hbm, em),
                (xm_hbm, xm),
                (emo_hbm, emo),
                (xmo_hbm, xmo),
                (esq_hbm, esq),
                (xsq_hbm, xsq),
                (cot_hbm, cot_v),
                (x_hbm, xc.at[:, pl.ds(0, feats)]),
                (dec_hbm.at[:, here], dec2),
                (dec_hbm, dec_v),
                (frz_hbm, frz_v),
            )
        )
    ]
    for load in loads:
        load.start()

    pack[0] = jnp.zeros(pack.shape[1:], F32)
    for i, (e_ref, o_ref) in enumerate(((em, xm), (emo, xmo), (esq, xsq))):
        loads[2 * i].wait()
        loads[2 * i + 1].wait()
        for p in range(2):
            for c in range(5):
                pack[0, i, p * 6 + c : p * 6 + c + 1, :] = e_ref[p, :, c * 128 : (c + 1) * 128]
            pack[0, i, p * 6 + 5 : p * 6 + 6, :] = o_ref[p, :, :]
    ga[0, s] = pack[0, 0].astype(BF)
    fac[...] = jnp.zeros_like(fac)
    xnew[...] = jnp.zeros_like(xnew)
    rs[...] = jnp.zeros_like(rs)
    loads[6].wait()
    wide[0 : 2 * tokens, :] = cot_v[...].astype(F32)
    for p in range(2):
        xc[:, feats + p * 128 : feats + (p + 1) * 128] = wide[pl.ds(p, tokens, stride=2), :].astype(BF)
    loads[7].wait()

    pl.semaphore_wait(barrier, len(peers))

    def spread_rows(stage, rows):
        for dp in near:
            send(stage, rows, rows, dp, t)

    send(1, ga.at[0, s], ga.at[1, s], partner, t)
    spread_rows(0, ga.at[0, s])
    send(17, pack.at[0], pack.at[1], partner, t)

    def project(half):
        wide[0 : group * 16, :] = ga[half].reshape(group * 16, 128).astype(F32)
        for p in range(2):
            for c in range(6):
                piece = wide[pl.ds(p * 6 + c, group, stride=16), :].astype(BF)
                if c < 5:
                    fac[half, p * group : (p + 1) * group, c * 128 : (c + 1) * 128] = piece
                else:
                    rows = slice((2 + p) * group, (3 + p) * group)
                    fac[half, rows, feats + p * 128 : feats + (p + 1) * 128] = piece
        lbf[half] = dot(xc[...], fac[half], 1, 1)
        lbs[half] = lbf[half].astype(BF).reshape(lbs.shape[1:])
        for k, tt in quad:
            send(3 + half, lbs.at[half, lax.rem(tt, quads)], l1.at[half, k - 1], me, tt)

    part = tokens // quads

    def sum_quad(half):
        if quads > 1:
            arrive(3 + half, l1.at[half])
        total = lbf[half, pl.ds(pl.multiple_of(ti * part, part), part), :]
        for k in range(quads - 1):
            total = total + l1[half, k].astype(F32)
        lbf[half, 0:part, :] = total
        l2s[half] = total.astype(BF)
        send(5 + half, l2s.at[half], l2.at[half], me, opposite)

    def sum_all(half):
        arrive(5 + half, l2.at[half])
        lfull[half, ti] = (lbf[half, 0:part, :] + l2[half].astype(F32)).astype(BF)
        for k, tt in quad:
            send(7 + half, lfull.at[half, ti], lfull.at[half, ti], me, tt)

    def gradients(half):
        if quads > 1:
            arrive(7 + half, lfull.at[half, pl.ds(0, quads - 1)])
        both = lfull[half].reshape(tokens, 4 * group)
        g = adapter_scale_factor * dot(both, xc[...], 0, 0)
        for p in range(2):
            for c in range(5):
                gr[half, pl.ds(p * 6 + c, group, stride=12), :] = g[
                    (2 + p) * group : (3 + p) * group, c * 128 : (c + 1) * 128
                ]
            gr[half, pl.ds(p * 6 + 5, group, stride=12), :] = g[
                p * group : (p + 1) * group, feats + p * 128 : feats + (p + 1) * 128
            ]
        for k, pp in plane:
            src = gr.at[half, pl.ds(pl.multiple_of(pp * 24, 24), 24)]
            send(9 + half, src, r1.at[half, k - 1], device(pp, zh, co), t)

    def sum_plane(half):
        if planes > 1:
            arrive(9 + half, r1.at[half])
        total = gr[half, pl.ds(pl.multiple_of(xy * 24, 24), 24), :]
        for k in range(planes - 1):
            total = total + r1[half, k]
        for c in range(2):
            rs[half, c, :12, :] = total[c * 12 : (c + 1) * 12, :]
        send(11 + half, rs.at[half, other_co], r2.at[half, 0], device(xy, zh, other_co), t)
        send(14 - half, rs.at[half, co], r2.at[1 - half, 1], partner, t)
        send(14 - half, rs.at[half, other_co], r2.at[1 - half, 2], cross, t)

    arrive(0, ga.at[0, pl.ds(0, group - 1)])
    project(0)
    arrive(1, ga.at[1, s])
    spread_rows(2, ga.at[1, s])
    sum_quad(0)
    arrive(2, ga.at[1, pl.ds(0, group - 1)])
    project(1)
    sum_all(0)
    sum_quad(1)
    gradients(0)
    sum_all(1)
    gradients(1)
    sum_plane(0)
    sum_plane(1)

    loads[8].wait()
    loads[9].wait()
    loads[10].wait()
    for p in range(2):
        base[:, p * 128 : (p + 1) * 128] = dot(dec_v[...], frz_v[p], 1, 0)

    arrive(17, pack.at[1])
    for half in (1, 0):
        arrive(11 + half, r2.at[half, 0])
        arrive(13 + half, r2.at[half, pl.ds(1, 2)])
        grad = (rs[half, co] + r2[half, 0]) + (r2[half, 1] + r2[half, 2])
        after, moment, square = adam_step(pack[half, 0], pack[half, 1], pack[half, 2], grad)
        gb[s, half] = after.astype(BF)
    spread_rows(15, gb.at[s])
    for i, value in enumerate((after, moment, square)):
        new_o[i] = value
    arrive(15, gb.at[pl.ds(0, group - 1)])

    wide[0 : group * 32, :] = gb[...].reshape(group * 32, 128).astype(F32)
    groups = [(slice((h * 2 + p) * group, (h * 2 + p + 1) * group), h, p) for h in range(2) for p in range(2)]
    for rows, h, p in groups:
        for c in range(5):
            piece = wide[pl.ds(h * 16 + p * 6 + c, group, stride=32), :].astype(BF)
            enew[rows, c * 128 : (c + 1) * 128] = piece
    inner = adapter_scale_factor * dot(dec2[...], enew[...], 1, 1)
    zs[...] = inner.astype(BF)
    for k, tt in tens:
        send(16, zs, zl.at[k - 1], me, tt)
    for rows, h, p in groups:
        piece = wide[pl.ds(h * 16 + p * 6 + 5, group, stride=32), :].astype(BF)
        xnew[rows, p * 128 : (p + 1) * 128] = piece
    arrive(16, zl)
    for k in range(nt - 1):
        inner = inner + zl[k].astype(F32)
    out = base[...] + dot(inner.astype(BF), xnew[...], 1, 0)
    rows = dec_v.shape[0]
    for p in range(2):
        wide[pl.ds(p, rows, stride=2), :] = out[:, p * 128 : (p + 1) * 128]
    proj_o[...] = wide[0 : 2 * rows, :].astype(BF)

    for stage, ref in sent:
        descriptor(stage, ref).wait_send()


def spread(new, proj, *rest):
    outs, parts, sem = rest[:7], rest[7:13], rest[13]
    copies = [pltpu.make_async_copy(proj, outs[0], sem.at[0])]
    copies[0].start()
    for i, (e, o) in enumerate(((0, 1), (2, 4), (3, 5))):
        for p in range(2):
            for c in range(5):
                row = p * 6 + c
                parts[e][p, :, c * 128 : (c + 1) * 128] = new[i, row : row + 1, :]
            parts[o][p, :, :] = new[i, p * 6 + 5 : p * 6 + 6, :]
        for n in (e, o):
            copies.append(pltpu.make_async_copy(parts[n], outs[n + 1], sem.at[n + 1]))
            copies[-1].start()
    for copy in copies:
        copy.wait()


def body(nx, ny, nt, x, cot, frz, dec, em, xm, emo, esq, xmo, xsq):
    tokens, feats = x.shape
    rows = dec.shape[0]
    planes = nx * ny
    group = planes * 2
    quads = nt // 2
    part = tokens // quads
    hbm = pl.BlockSpec(memory_space=pltpu.HBM)
    vmem = pl.BlockSpec(memory_space=pltpu.VMEM)
    like = lambda a: jax.ShapeDtypeStruct(a.shape, a.dtype)
    held = lambda a: pltpu.VMEM(a.shape, a.dtype)
    proj, new = pl.pallas_call(
        functools.partial(kernel, nx, ny, nt),
        out_shape=(
            jax.ShapeDtypeStruct((rows * 2, 128), BF),
            jax.ShapeDtypeStruct((3, 16, 128), F32),
        ),
        in_specs=[hbm] * 10,
        out_specs=[vmem] * 2,
        scratch_shapes=[
            held(em), held(xm), held(em), held(xm), held(em), held(xm),
            pltpu.VMEM((tokens, feats + 256), BF),
            pltpu.VMEM((tokens * 2, 128), BF),
            held(frz),
            held(dec),
            pltpu.VMEM((rows, feats), BF),
            pltpu.VMEM((max(2 * tokens, group * 32), 128), F32),
            pltpu.VMEM((rows, 256), F32),
            pltpu.VMEM((2, 3, 16, 128), F32),
            pltpu.VMEM((2, group, 16, 128), BF),
            pltpu.VMEM((group, 2, 16, 128), BF),
            pltpu.VMEM((2, 4 * group, feats + 256), BF),
            pltpu.VMEM((4 * group, feats), BF),
            pltpu.VMEM((4 * group, 256), BF),
            pltpu.VMEM((2, tokens, 4 * group), F32),
            pltpu.VMEM((2, quads, part, 4 * group), BF),
            pltpu.VMEM((2, max(quads - 1, 1), part, 4 * group), BF),
            pltpu.VMEM((2, part, 4 * group), BF),
            pltpu.VMEM((2, part, 4 * group), BF),
            pltpu.VMEM((2, quads, part, 4 * group), BF),
            pltpu.VMEM((2, group * 12, 128), F32),
            pltpu.VMEM((2, max(planes - 1, 1), 24, 128), F32),
            pltpu.VMEM((2, 2, 16, 128), F32),
            pltpu.VMEM((2, 3, 16, 128), F32),
            pltpu.VMEM((rows, 4 * group), BF),
            pltpu.VMEM((nt - 1, rows, 4 * group), BF),
            pltpu.SemaphoreType.DMA((11,)),
            pltpu.SemaphoreType.DMA((18,)),
            pltpu.SemaphoreType.DMA((18,)),
        ],
        compiler_params=pltpu.CompilerParams(
            collective_id=0, has_side_effects=True, vmem_limit_bytes=63 * 1024 * 1024
        ),
        cost_estimate=pl.CostEstimate(flops=600_000_000, bytes_accessed=5_000_000, transcendentals=0),
    )(x, cot.reshape(tokens * 2, 128), frz, dec, em, xm, emo, esq, xmo, xsq)
    factors = [em, xm, em, em, xm, xm]
    out = pl.pallas_call(
        spread,
        out_shape=(like(proj),) + tuple(like(f) for f in factors),
        in_specs=[vmem] * 2,
        out_specs=[hbm] * 7,
        scratch_shapes=[held(f) for f in factors] + [pltpu.SemaphoreType.DMA((7,))],
        cost_estimate=pl.CostEstimate(flops=10_000, bytes_accessed=60_000, transcendentals=0),
    )(new, proj)
    return (out[0].reshape(rows, 2, 128),) + tuple(out[1:])


def solution(mesh):
    nt = mesh.shape["tensor"]
    planes = mesh.shape["dp"] // QUAD
    ny = min(planes, 4)
    nx = planes // ny
    factor = P(None, "dp", "tensor")
    return jax.shard_map(
        functools.partial(body, nx, ny, nt),
        mesh=mesh,
        in_specs=(
            P("dp", "tensor"),
            P("dp", None, "tensor"),
            P(None, None, "tensor"),
            P("dp", None),
        )
        + (factor,) * 6,
        out_specs=(P("dp", None, "tensor"),) + (factor,) * 6,
        check_vma=False,
    )
```

```python
import functools

import jax
import jax.numpy as jnp
from jax import lax
from jax.experimental import pallas as pl
from jax.experimental.pallas import tpu as pltpu
from jax.sharding import PartitionSpec as P

adapter_scale_factor = 2.0
beta_first = 0.9
beta_second = 0.999
correct_first = 1.0 - 0.9**10
correct_second = 1.0 - 0.999**10
learn_rate = 0.002
decay_rate = 0.01
epsilon = 1e-08

BF = jnp.bfloat16
F32 = jnp.float32
QUAD = 4


def adam_step(master, moment, square, grad):
    moment_new = beta_first * moment + (1.0 - beta_first) * grad
    square_new = beta_second * square + (1.0 - beta_second) * grad * grad
    update = moment_new / correct_first / (jnp.sqrt(square_new / correct_second) + epsilon)
    return (master - learn_rate * (update + decay_rate * master), moment_new, square_new)


def dot(a, b, ca, cb):
    return lax.dot_general(a, b, (((ca,), (cb,)), ((), ())), preferred_element_type=F32)


def kernel(
    nx, ny, nt,
    x_hbm, cot_hbm, frz_hbm, dec_hbm, em_hbm, xm_hbm, emo_hbm, esq_hbm, xmo_hbm, xsq_hbm,
    proj_o, new_o,
    em, xm, emo, xmo, esq, xsq, xc, cot_v, frz_v, dec_v, dec2, wide, base,
    pack, ga, gb, fac, enew, xnew, lbf, lbs, l1, l2s, l2, lfull,
    gr, r1, rs, r2, zs, zl, zx,
    local_sem, send_sem, recv_sem,
):
    planes = nx * ny
    group = planes * 2
    quads = nt // 2
    tokens = xc.shape[0]
    feats = em_hbm.shape[2]
    me = lax.axis_index("dp")
    t = lax.axis_index("tensor")
    xy = lax.div(me, QUAD)
    q = lax.rem(me, QUAD)
    xi, yi = lax.div(xy, ny), lax.rem(xy, ny)
    zh, co = lax.div(q, 2), lax.rem(q, 2)
    tq, ti = lax.div(t, quads), lax.rem(t, quads)
    s = xy * 2 + co

    def plane_peer(k):
        return lax.rem(xi + k // ny, nx) * ny + lax.rem(yi + k % ny, ny)

    def device(pp, z, c):
        return pp * QUAD + z * 2 + c

    other_zh, other_co = 1 - zh, 1 - co
    order = sorted(
        range(1, planes), key=lambda k: -(min(k // ny, nx - k // ny) + min(k % ny, ny - k % ny))
    )
    plane = [(k, plane_peer(k)) for k in order]
    near = [device(pp, zh, c) for _, pp in plane for c in (co, other_co)]
    near.append(device(xy, zh, other_co))
    partner = device(xy, other_zh, co)
    cross = device(xy, other_zh, other_co)
    ring = sorted(range(1, nt), key=lambda k: abs(k - nt // 2))
    tens = [(k, lax.rem(t + k, nt)) for k in ring]
    far = [0] + ring[::-1]
    quad = [(k, tq * quads + lax.rem(ti + k, quads)) for k in range(1, quads)]
    opposite = (1 - tq) * quads + ti

    def send(stage, src, dst, dp, tn):
        pltpu.make_async_remote_copy(
            src_ref=src, dst_ref=dst, send_sem=send_sem.at[stage], recv_sem=recv_sem.at[stage],
            device_id=(dp, tn), device_id_type=pl.DeviceIdType.MESH,
        ).start()

    def descriptor(stage, ref):
        return pltpu.make_async_remote_copy(
            src_ref=ref, dst_ref=ref, send_sem=send_sem.at[stage], recv_sem=recv_sem.at[stage],
            device_id=(partner, t), device_id_type=pl.DeviceIdType.MESH,
        )

    sent = []

    def arrive(stage, ref):
        descriptor(stage, ref).wait_recv()
        sent.append((stage, ref))

    barrier = pltpu.get_barrier_semaphore()
    peers = [(partner, t), (cross, t)] + [(dp, t) for dp in near]
    peers += [(dp, tt) for _, tt in tens for dp in (me, partner)]
    for peer in peers:
        pl.semaphore_signal(barrier, inc=1, device_id=peer, device_id_type=pl.DeviceIdType.MESH)

    here = pl.ds(pl.multiple_of(t * feats, feats), feats)
    loads = [
        pltpu.make_async_copy(src, dst, local_sem.at[i])
        for i, (src, dst) in enumerate(
            (
                (em_hbm, em),
                (xm_hbm, xm),
                (emo_hbm, emo),
                (xmo_hbm, xmo),
                (esq_hbm, esq),
                (xsq_hbm, xsq),
                (cot_hbm, cot_v),
                (x_hbm, xc.at[:, pl.ds(0, feats)]),
                (dec_hbm.at[:, here], dec2.at[0]),
                (dec_hbm, dec_v),
                (frz_hbm, frz_v),
            )
        )
    ]
    for load in loads:
        load.start()

    pack[0] = jnp.zeros(pack.shape[1:], F32)
    for i, (e_ref, o_ref) in enumerate(((em, xm), (emo, xmo), (esq, xsq))):
        loads[2 * i].wait()
        loads[2 * i + 1].wait()
        for p in range(2):
            for c in range(5):
                pack[0, i, p * 6 + c : p * 6 + c + 1, :] = e_ref[p, :, c * 128 : (c + 1) * 128]
            pack[0, i, p * 6 + 5 : p * 6 + 6, :] = o_ref[p, :, :]
    ga[0, s] = pack[0, 0].astype(BF)
    fac[...] = jnp.zeros_like(fac)
    xnew[...] = jnp.zeros_like(xnew)
    rs[...] = jnp.zeros_like(rs)
    loads[6].wait()
    wide[0 : 2 * tokens, :] = cot_v[...].astype(F32)
    for p in range(2):
        xc[:, feats + p * 128 : feats + (p + 1) * 128] = wide[pl.ds(p, tokens, stride=2), :].astype(BF)
    loads[7].wait()
    loads[8].wait()

    pl.semaphore_wait(barrier, len(peers))

    def spread_rows(stage, rows):
        for dp in near:
            send(stage, rows, rows, dp, t)

    send(1, ga.at[0, s], ga.at[1, s], partner, t)
    spread_rows(0, ga.at[0, s])
    send(17, pack.at[0], pack.at[1], partner, t)
    half_rows = dec_v.shape[0] // 2

    def send_decode(part):
        these = pl.ds(part * half_rows, half_rows)
        send(18, dec2.at[0, these], dec2.at[1, these], partner, t)

    send_decode(0)

    def project(half):
        wide[0 : group * 16, :] = ga[half].reshape(group * 16, 128).astype(F32)
        for p in range(2):
            for c in range(6):
                piece = wide[pl.ds(p * 6 + c, group, stride=16), :].astype(BF)
                if c < 5:
                    fac[half, p * group : (p + 1) * group, c * 128 : (c + 1) * 128] = piece
                else:
                    rows = slice((2 + p) * group, (3 + p) * group)
                    fac[half, rows, feats + p * 128 : feats + (p + 1) * 128] = piece
        lbf[half] = dot(xc[...], fac[half], 1, 1)
        lbs[half] = lbf[half].astype(BF).reshape(lbs.shape[1:])
        for k, tt in quad:
            send(3 + half, lbs.at[half, lax.rem(tt, quads)], l1.at[half, k - 1], me, tt)

    part = tokens // quads

    def sum_quad(half):
        if quads > 1:
            arrive(3 + half, l1.at[half])
        total = lbf[half, pl.ds(pl.multiple_of(ti * part, part), part), :]
        for k in range(quads - 1):
            total = total + l1[half, k].astype(F32)
        lbf[half, 0:part, :] = total
        l2s[half] = total.astype(BF)
        send(5 + half, l2s.at[half], l2.at[half], me, opposite)

    def sum_all(half):
        arrive(5 + half, l2.at[half])
        lfull[half, ti] = (lbf[half, 0:part, :] + l2[half].astype(F32)).astype(BF)
        for k, tt in quad:
            send(7 + half, lfull.at[half, ti], lfull.at[half, ti], me, tt)

    def gradients(half):
        if quads > 1:
            arrive(7 + half, lfull.at[half, pl.ds(0, quads - 1)])
        both = lfull[half].reshape(tokens, 4 * group)
        g = adapter_scale_factor * dot(both, xc[...], 0, 0)
        for p in range(2):
            for c in range(5):
                gr[half, pl.ds(p * 6 + c, group, stride=12), :] = g[
                    (2 + p) * group : (3 + p) * group, c * 128 : (c + 1) * 128
                ]
            gr[half, pl.ds(p * 6 + 5, group, stride=12), :] = g[
                p * group : (p + 1) * group, feats + p * 128 : feats + (p + 1) * 128
            ]
        for k, pp in plane:
            src = gr.at[half, pl.ds(pl.multiple_of(pp * 24, 24), 24)]
            send(9 + half, src, r1.at[half, k - 1], device(pp, zh, co), t)

    def sum_plane(half):
        if planes > 1:
            arrive(9 + half, r1.at[half])
        total = gr[half, pl.ds(pl.multiple_of(xy * 24, 24), 24), :]
        for k in range(planes - 1):
            total = total + r1[half, k]
        for c in range(2):
            rs[half, c, :12, :] = total[c * 12 : (c + 1) * 12, :]
        send(11 + half, rs.at[half, other_co], r2.at[half, 0], device(xy, zh, other_co), t)
        send(14 - half, rs.at[half, co], r2.at[1 - half, 1], partner, t)
        send(14 - half, rs.at[half, other_co], r2.at[1 - half, 2], cross, t)

    arrive(0, ga.at[0, pl.ds(0, group - 1)])
    project(0)
    arrive(1, ga.at[1, s])
    spread_rows(2, ga.at[1, s])
    sum_quad(0)
    arrive(2, ga.at[1, pl.ds(0, group - 1)])
    project(1)
    sum_all(0)
    sum_quad(1)
    gradients(0)
    sum_all(1)
    send_decode(1)
    gradients(1)
    sum_plane(0)
    loads[9].wait()
    loads[10].wait()
    for p in range(2):
        base[:, p * 128 : (p + 1) * 128] = dot(dec_v[...], frz_v[p], 1, 0)

    sum_plane(1)

    def update(half):
        arrive(11 + half, r2.at[half, 0])
        arrive(13 + half, r2.at[half, pl.ds(1, 2)])
        grad = (rs[half, co] + r2[half, 0]) + (r2[half, 1] + r2[half, 2])
        return adam_step(pack[half, 0], pack[half, 1], pack[half, 2], grad)

    def unpack_new(half, pieces):
        wide[0 : group * 16, :] = gb[half].reshape(group * 16, 128).astype(F32)
        for p in range(2):
            for c in pieces:
                piece = wide[pl.ds(p * 6 + c, group, stride=16), :].astype(BF)
                if c < 5:
                    enew[p * group : (p + 1) * group, c * 128 : (c + 1) * 128] = piece
                else:
                    rows = slice((half * 2 + p) * group, (half * 2 + p + 1) * group)
                    xnew[rows, p * 128 : (p + 1) * 128] = piece

    arrive(17, pack.at[1])
    gb[1, s] = update(1)[0].astype(BF)
    spread_rows(15, gb.at[1, s])
    arrive(18, dec2.at[1])
    arrive(15, gb.at[1, pl.ds(0, group - 1)])
    unpack_new(1, range(5))
    inner = [adapter_scale_factor * dot(dec2[i], enew[...], 1, 1) for i in (1, 0)]
    inner = [jnp.concatenate([v[:half_rows], v[half_rows:]], axis=1) for v in inner]
    for i in range(2):
        zs[i] = inner[i].astype(BF)
    for k in far:
        send(20, zs.at[0], zx.at[k], partner, lax.rem(t + k, nt))
    for k, tt in tens:
        send(16, zs.at[1], zl.at[k - 1], me, tt)
    unpack_new(1, (5,))

    after, moment, square = update(0)
    gb[0, s] = after.astype(BF)
    spread_rows(19, gb.at[0, s])
    for i, value in enumerate((after, moment, square)):
        new_o[i] = value
    arrive(19, gb.at[0, pl.ds(0, group - 1)])
    unpack_new(0, (5,))

    arrive(16, zl)
    arrive(20, zx)
    own, other = zx[0].astype(F32), inner[1]
    for k in range(nt - 1):
        own = own + zx[k + 1].astype(F32)
        other = other + zl[k].astype(F32)
    both = jnp.concatenate(
        [
            jnp.concatenate([v[:, : 2 * group], v[:, 2 * group :]], axis=0)
            for v in (own.astype(BF), other.astype(BF))
        ],
        axis=1,
    )
    out = base[...] + dot(both, xnew[...], 1, 0)
    rows = 2 * half_rows
    for p in range(2):
        wide[pl.ds(p, rows, stride=2), :] = out[:, p * 128 : (p + 1) * 128]
    proj_o[...] = wide[0 : 2 * rows, :].astype(BF)

    for stage, ref in sent:
        descriptor(stage, ref).wait_send()


def spread(new, proj, *rest):
    outs, parts, sem = rest[:7], rest[7:13], rest[13]
    copies = [pltpu.make_async_copy(proj, outs[0], sem.at[0])]
    copies[0].start()
    for i, (e, o) in enumerate(((0, 1), (2, 4), (3, 5))):
        for p in range(2):
            for c in range(5):
                row = p * 6 + c
                parts[e][p, :, c * 128 : (c + 1) * 128] = new[i, row : row + 1, :]
            parts[o][p, :, :] = new[i, p * 6 + 5 : p * 6 + 6, :]
        for n in (e, o):
            copies.append(pltpu.make_async_copy(parts[n], outs[n + 1], sem.at[n + 1]))
            copies[-1].start()
    for copy in copies:
        copy.wait()


def body(nx, ny, nt, x, cot, frz, dec, em, xm, emo, esq, xmo, xsq):
    tokens, feats = x.shape
    rows = dec.shape[0]
    planes = nx * ny
    group = planes * 2
    quads = nt // 2
    part = tokens // quads
    hbm = pl.BlockSpec(memory_space=pltpu.HBM)
    vmem = pl.BlockSpec(memory_space=pltpu.VMEM)
    like = lambda a: jax.ShapeDtypeStruct(a.shape, a.dtype)
    held = lambda a: pltpu.VMEM(a.shape, a.dtype)
    proj, new = pl.pallas_call(
        functools.partial(kernel, nx, ny, nt),
        out_shape=(
            jax.ShapeDtypeStruct((rows * 2, 128), BF),
            jax.ShapeDtypeStruct((3, 16, 128), F32),
        ),
        in_specs=[hbm] * 10,
        out_specs=[vmem] * 2,
        scratch_shapes=[
            held(em), held(xm), held(em), held(xm), held(em), held(xm),
            pltpu.VMEM((tokens, feats + 256), BF),
            pltpu.VMEM((tokens * 2, 128), BF),
            held(frz),
            held(dec),
            pltpu.VMEM((2, rows, feats), BF),
            pltpu.VMEM((max(2 * tokens, group * 16), 128), F32),
            pltpu.VMEM((rows, 256), F32),
            pltpu.VMEM((2, 3, 16, 128), F32),
            pltpu.VMEM((2, group, 16, 128), BF),
            pltpu.VMEM((2, group, 16, 128), BF),
            pltpu.VMEM((2, 4 * group, feats + 256), BF),
            pltpu.VMEM((2 * group, feats), BF),
            pltpu.VMEM((4 * group, 256), BF),
            pltpu.VMEM((2, tokens, 4 * group), F32),
            pltpu.VMEM((2, quads, part, 4 * group), BF),
            pltpu.VMEM((2, max(quads - 1, 1), part, 4 * group), BF),
            pltpu.VMEM((2, part, 4 * group), BF),
            pltpu.VMEM((2, part, 4 * group), BF),
            pltpu.VMEM((2, quads, part, 4 * group), BF),
            pltpu.VMEM((2, group * 12, 128), F32),
            pltpu.VMEM((2, max(planes - 1, 1), 24, 128), F32),
            pltpu.VMEM((2, 2, 16, 128), F32),
            pltpu.VMEM((2, 3, 16, 128), F32),
            pltpu.VMEM((2, rows // 2, 4 * group), BF),
            pltpu.VMEM((nt - 1, rows // 2, 4 * group), BF),
            pltpu.VMEM((nt, rows // 2, 4 * group), BF),
            pltpu.SemaphoreType.DMA((11,)),
            pltpu.SemaphoreType.DMA((21,)),
            pltpu.SemaphoreType.DMA((21,)),
        ],
        compiler_params=pltpu.CompilerParams(
            collective_id=0, has_side_effects=True, vmem_limit_bytes=63 * 1024 * 1024
        ),
        cost_estimate=pl.CostEstimate(flops=600_000_000, bytes_accessed=5_000_000, transcendentals=0),
    )(x, cot.reshape(tokens * 2, 128), frz, dec, em, xm, emo, esq, xmo, xsq)
    factors = [em, xm, em, em, xm, xm]
    out = pl.pallas_call(
        spread,
        out_shape=(like(proj),) + tuple(like(f) for f in factors),
        in_specs=[vmem] * 2,
        out_specs=[hbm] * 7,
        scratch_shapes=[held(f) for f in factors] + [pltpu.SemaphoreType.DMA((7,))],
        cost_estimate=pl.CostEstimate(flops=10_000, bytes_accessed=60_000, transcendentals=0),
    )(new, proj)
    return (out[0].reshape(rows, 2, 128),) + tuple(out[1:])


def solution(mesh):
    nt = mesh.shape["tensor"]
    planes = mesh.shape["dp"] // QUAD
    ny = min(planes, 4)
    nx = planes // ny
    factor = P(None, "dp", "tensor")
    return jax.shard_map(
        functools.partial(body, nx, ny, nt),
        mesh=mesh,
        in_specs=(
            P("dp", "tensor"),
            P("dp", None, "tensor"),
            P(None, None, "tensor"),
            P("dp", None),
        )
        + (factor,) * 6,
        out_specs=(P("dp", None, "tensor"),) + (factor,) * 6,
        check_vma=False,
    )
```

```python
import functools

import jax
import jax.numpy as jnp
from jax import lax
from jax.experimental import pallas as pl
from jax.experimental.pallas import tpu as pltpu
from jax.sharding import PartitionSpec as P

adapter_scale_factor = 2.0
beta_first = 0.9
beta_second = 0.999
correct_first = 1.0 - 0.9**10
correct_second = 1.0 - 0.999**10
learn_rate = 0.002
decay_rate = 0.01
epsilon = 1e-08

BF = jnp.bfloat16
F32 = jnp.float32
QUAD = 4


def adam_step(master, moment, square, grad):
    moment_new = beta_first * moment + (1.0 - beta_first) * grad
    square_new = beta_second * square + (1.0 - beta_second) * grad * grad
    update = moment_new / correct_first / (jnp.sqrt(square_new / correct_second) + epsilon)
    return (master - learn_rate * (update + decay_rate * master), moment_new, square_new)


def dot(a, b, ca, cb):
    return lax.dot_general(a, b, (((ca,), (cb,)), ((), ())), preferred_element_type=F32)


def kernel(
    nx, ny, nt,
    x_hbm, cot_hbm, frz_hbm, dec_hbm, em_hbm, xm_hbm, emo_hbm, esq_hbm, xmo_hbm, xsq_hbm,
    proj_o, new_o,
    em, xm, emo, xmo, esq, xsq, xc, cot_v, frz_v, dec_v, dec2, wide, base,
    pack, ga, gb, fac, enew, xnew, lbf, lbs, l1, l2s, l2, lfull,
    gr, r1, rs, r2, zs, zl, zx,
    local_sem, send_sem, recv_sem,
):
    planes = nx * ny
    group = planes * 2
    quads = nt // 2
    tokens = xc.shape[0]
    feats = em_hbm.shape[2]
    me = lax.axis_index("dp")
    t = lax.axis_index("tensor")
    xy = lax.div(me, QUAD)
    q = lax.rem(me, QUAD)
    xi, yi = lax.div(xy, ny), lax.rem(xy, ny)
    zh, co = lax.div(q, 2), lax.rem(q, 2)
    tq, ti = lax.div(t, quads), lax.rem(t, quads)
    s = xy * 2 + co

    def plane_peer(k):
        return lax.rem(xi + k // ny, nx) * ny + lax.rem(yi + k % ny, ny)

    def device(pp, z, c):
        return pp * QUAD + z * 2 + c

    other_zh, other_co = 1 - zh, 1 - co
    order = sorted(
        range(1, planes), key=lambda k: -(min(k // ny, nx - k // ny) + min(k % ny, ny - k % ny))
    )
    plane = [(k, plane_peer(k)) for k in order]
    near = [device(pp, zh, c) for _, pp in plane for c in (co, other_co)]
    near.append(device(xy, zh, other_co))
    partner = device(xy, other_zh, co)
    cross = device(xy, other_zh, other_co)
    ring = sorted(range(1, nt), key=lambda k: abs(k - nt // 2))
    tens = [(k, lax.rem(t + k, nt)) for k in ring]
    far = [0] + ring[::-1]
    quad = [(k, tq * quads + lax.rem(ti + k, quads)) for k in range(1, quads)]
    opposite = (1 - tq) * quads + ti

    def send(stage, src, dst, dp, tn):
        pltpu.make_async_remote_copy(
            src_ref=src, dst_ref=dst, send_sem=send_sem.at[stage], recv_sem=recv_sem.at[stage],
            device_id=(dp, tn), device_id_type=pl.DeviceIdType.MESH,
        ).start()

    def descriptor(stage, ref):
        return pltpu.make_async_remote_copy(
            src_ref=ref, dst_ref=ref, send_sem=send_sem.at[stage], recv_sem=recv_sem.at[stage],
            device_id=(partner, t), device_id_type=pl.DeviceIdType.MESH,
        )

    sent = []

    def arrive(stage, ref):
        descriptor(stage, ref).wait_recv()
        sent.append((stage, ref))

    barrier = pltpu.get_barrier_semaphore()
    peers = [(partner, t), (cross, t)] + [(dp, t) for dp in near]
    peers += [(dp, tt) for _, tt in tens for dp in (me, partner)]
    for peer in peers:
        pl.semaphore_signal(barrier, inc=1, device_id=peer, device_id_type=pl.DeviceIdType.MESH)

    here = pl.ds(pl.multiple_of(t * feats, feats), feats)
    loads = [
        pltpu.make_async_copy(src, dst, local_sem.at[i])
        for i, (src, dst) in enumerate(
            (
                (em_hbm, em),
                (xm_hbm, xm),
                (emo_hbm, emo),
                (xmo_hbm, xmo),
                (esq_hbm, esq),
                (xsq_hbm, xsq),
                (cot_hbm, cot_v),
                (x_hbm, xc.at[:, pl.ds(0, feats)]),
                (dec_hbm.at[:, here], dec2.at[0]),
                (dec_hbm, dec_v),
                (frz_hbm, frz_v),
            )
        )
    ]
    for load in loads:
        load.start()

    pack[0] = jnp.zeros(pack.shape[1:], F32)
    for i, (e_ref, o_ref) in enumerate(((em, xm), (emo, xmo), (esq, xsq))):
        loads[2 * i].wait()
        loads[2 * i + 1].wait()
        for p in range(2):
            for c in range(5):
                pack[0, i, p * 6 + c : p * 6 + c + 1, :] = e_ref[p, :, c * 128 : (c + 1) * 128]
            pack[0, i, p * 6 + 5 : p * 6 + 6, :] = o_ref[p, :, :]
    ga[0, s] = pack[0, 0].astype(BF)
    fac[...] = jnp.zeros_like(fac)
    xnew[...] = jnp.zeros_like(xnew)
    rs[...] = jnp.zeros_like(rs)
    loads[6].wait()
    wide[0 : 2 * tokens, :] = cot_v[...].astype(F32)
    for p in range(2):
        xc[:, feats + p * 128 : feats + (p + 1) * 128] = wide[pl.ds(p, tokens, stride=2), :].astype(BF)
    loads[7].wait()
    loads[8].wait()

    pl.semaphore_wait(barrier, len(peers))

    def spread_rows(stage, rows):
        for dp in near:
            send(stage, rows, rows, dp, t)

    send(1, ga.at[0, s], ga.at[1, s], partner, t)
    spread_rows(0, ga.at[0, s])
    send(17, pack.at[0], pack.at[1], partner, t)
    half_rows = dec_v.shape[0] // 2

    def send_decode(first, count):
        these = pl.ds(first, count)
        send(18, dec2.at[0, these], dec2.at[1, these], partner, t)

    send_decode(0, half_rows)

    def project(half):
        wide[0 : group * 16, :] = ga[half].reshape(group * 16, 128).astype(F32)
        for p in range(2):
            for c in range(6):
                piece = wide[pl.ds(p * 6 + c, group, stride=16), :].astype(BF)
                if c < 5:
                    fac[half, p * group : (p + 1) * group, c * 128 : (c + 1) * 128] = piece
                else:
                    rows = slice((2 + p) * group, (3 + p) * group)
                    fac[half, rows, feats + p * 128 : feats + (p + 1) * 128] = piece
        lbf[half] = dot(xc[...], fac[half], 1, 1)
        lbs[half] = lbf[half].astype(BF).reshape(lbs.shape[1:])
        for k, tt in quad:
            send(3 + half, lbs.at[half, lax.rem(tt, quads)], l1.at[half, k - 1], me, tt)

    part = tokens // quads

    def sum_quad(half):
        if quads > 1:
            arrive(3 + half, l1.at[half])
        total = lbf[half, pl.ds(pl.multiple_of(ti * part, part), part), :]
        for k in range(quads - 1):
            total = total + l1[half, k].astype(F32)
        lbf[half, 0:part, :] = total
        l2s[half] = total.astype(BF)
        send(5 + half, l2s.at[half], l2.at[half], me, opposite)

    def sum_all(half):
        arrive(5 + half, l2.at[half])
        lfull[half, ti] = (lbf[half, 0:part, :] + l2[half].astype(F32)).astype(BF)
        for k, tt in quad:
            send(7 + half, lfull.at[half, ti], lfull.at[half, ti], me, tt)

    def gradients(half):
        if quads > 1:
            arrive(7 + half, lfull.at[half, pl.ds(0, quads - 1)])
        if half == 1:
            send_decode(half_rows, half_rows)
        both = lfull[half].reshape(tokens, 4 * group)
        g = adapter_scale_factor * dot(both, xc[...], 0, 0)
        for p in range(2):
            for c in range(5):
                gr[half, pl.ds(p * 6 + c, group, stride=12), :] = g[
                    (2 + p) * group : (3 + p) * group, c * 128 : (c + 1) * 128
                ]
            gr[half, pl.ds(p * 6 + 5, group, stride=12), :] = g[
                p * group : (p + 1) * group, feats + p * 128 : feats + (p + 1) * 128
            ]
        for k, pp in plane:
            src = gr.at[half, pl.ds(pl.multiple_of(pp * 24, 24), 24)]
            send(9 + half, src, r1.at[half, k - 1], device(pp, zh, co), t)

    def sum_plane(half):
        if planes > 1:
            arrive(9 + half, r1.at[half])
        total = gr[half, pl.ds(pl.multiple_of(xy * 24, 24), 24), :]
        for k in range(planes - 1):
            total = total + r1[half, k]
        for c in range(2):
            rs[half, c, :12, :] = total[c * 12 : (c + 1) * 12, :]
        send(11 + half, rs.at[half, other_co], r2.at[half, 0], device(xy, zh, other_co), t)
        send(14 - half, rs.at[half, co], r2.at[1 - half, 1], partner, t)
        send(14 - half, rs.at[half, other_co], r2.at[1 - half, 2], cross, t)

    arrive(0, ga.at[0, pl.ds(0, group - 1)])
    project(0)
    arrive(1, ga.at[1, s])
    spread_rows(2, ga.at[1, s])
    sum_quad(0)
    arrive(2, ga.at[1, pl.ds(0, group - 1)])
    project(1)
    sum_all(0)
    sum_quad(1)
    gradients(0)
    sum_all(1)
    sum_plane(0)
    gradients(1)
    loads[9].wait()
    loads[10].wait()
    for p in range(2):
        base[:, p * 128 : (p + 1) * 128] = dot(dec_v[...], frz_v[p], 1, 0)

    sum_plane(1)

    def update(half):
        arrive(11 + half, r2.at[half, 0])
        arrive(13 + half, r2.at[half, pl.ds(1, 2)])
        grad = (rs[half, co] + r2[half, 0]) + (r2[half, 1] + r2[half, 2])
        return adam_step(pack[half, 0], pack[half, 1], pack[half, 2], grad)

    def unpack_new(half, pieces):
        wide[0 : group * 16, :] = gb[half].reshape(group * 16, 128).astype(F32)
        for p in range(2):
            for c in pieces:
                piece = wide[pl.ds(p * 6 + c, group, stride=16), :].astype(BF)
                if c < 5:
                    enew[p * group : (p + 1) * group, c * 128 : (c + 1) * 128] = piece
                else:
                    rows = slice((half * 2 + p) * group, (half * 2 + p + 1) * group)
                    xnew[rows, p * 128 : (p + 1) * 128] = piece

    arrive(17, pack.at[1])
    gb[1, s] = update(1)[0].astype(BF)
    spread_rows(15, gb.at[1, s])
    arrive(18, dec2.at[1])
    arrive(15, gb.at[1, pl.ds(0, group - 1)])
    unpack_new(1, range(5))
    inner = [adapter_scale_factor * dot(dec2[i], enew[...], 1, 1) for i in (1, 0)]
    inner = [jnp.concatenate([v[:half_rows], v[half_rows:]], axis=1) for v in inner]
    for i in range(2):
        zs[i] = inner[i].astype(BF)
    for k in far:
        send(20, zs.at[0], zx.at[k], partner, lax.rem(t + k, nt))
    for k, tt in tens:
        send(16, zs.at[1], zl.at[k - 1], me, tt)
    unpack_new(1, (5,))

    after, moment, square = update(0)
    gb[0, s] = after.astype(BF)
    spread_rows(19, gb.at[0, s])
    for i, value in enumerate((after, moment, square)):
        new_o[i] = value
    arrive(19, gb.at[0, pl.ds(0, group - 1)])
    unpack_new(0, (5,))

    arrive(16, zl)
    arrive(20, zx)
    own, other = zx[0].astype(F32), inner[1]
    for k in range(nt - 1):
        own = own + zx[k + 1].astype(F32)
        other = other + zl[k].astype(F32)
    both = jnp.concatenate(
        [
            jnp.concatenate([v[:, : 2 * group], v[:, 2 * group :]], axis=0)
            for v in (own.astype(BF), other.astype(BF))
        ],
        axis=1,
    )
    out = base[...] + dot(both, xnew[...], 1, 0)
    rows = 2 * half_rows
    for p in range(2):
        wide[pl.ds(p, rows, stride=2), :] = out[:, p * 128 : (p + 1) * 128]
    proj_o[...] = wide[0 : 2 * rows, :].astype(BF)

    for stage, ref in sent:
        descriptor(stage, ref).wait_send()


def spread(new, proj, *rest):
    outs, parts, sem = rest[:7], rest[7:13], rest[13]
    copies = [pltpu.make_async_copy(proj, outs[0], sem.at[0])]
    copies[0].start()
    for i, (e, o) in enumerate(((0, 1), (2, 4), (3, 5))):
        for p in range(2):
            for c in range(5):
                row = p * 6 + c
                parts[e][p, :, c * 128 : (c + 1) * 128] = new[i, row : row + 1, :]
            parts[o][p, :, :] = new[i, p * 6 + 5 : p * 6 + 6, :]
        for n in (e, o):
            copies.append(pltpu.make_async_copy(parts[n], outs[n + 1], sem.at[n + 1]))
            copies[-1].start()
    for copy in copies:
        copy.wait()


def body(nx, ny, nt, x, cot, frz, dec, em, xm, emo, esq, xmo, xsq):
    tokens, feats = x.shape
    rows = dec.shape[0]
    planes = nx * ny
    group = planes * 2
    quads = nt // 2
    part = tokens // quads
    hbm = pl.BlockSpec(memory_space=pltpu.HBM)
    vmem = pl.BlockSpec(memory_space=pltpu.VMEM)
    like = lambda a: jax.ShapeDtypeStruct(a.shape, a.dtype)
    held = lambda a: pltpu.VMEM(a.shape, a.dtype)
    proj, new = pl.pallas_call(
        functools.partial(kernel, nx, ny, nt),
        out_shape=(
            jax.ShapeDtypeStruct((rows * 2, 128), BF),
            jax.ShapeDtypeStruct((3, 16, 128), F32),
        ),
        in_specs=[hbm] * 10,
        out_specs=[vmem] * 2,
        scratch_shapes=[
            held(em), held(xm), held(em), held(xm), held(em), held(xm),
            pltpu.VMEM((tokens, feats + 256), BF),
            pltpu.VMEM((tokens * 2, 128), BF),
            held(frz),
            held(dec),
            pltpu.VMEM((2, rows, feats), BF),
            pltpu.VMEM((max(2 * tokens, group * 16), 128), F32),
            pltpu.VMEM((rows, 256), F32),
            pltpu.VMEM((2, 3, 16, 128), F32),
            pltpu.VMEM((2, group, 16, 128), BF),
            pltpu.VMEM((2, group, 16, 128), BF),
            pltpu.VMEM((2, 4 * group, feats + 256), BF),
            pltpu.VMEM((2 * group, feats), BF),
            pltpu.VMEM((4 * group, 256), BF),
            pltpu.VMEM((2, tokens, 4 * group), F32),
            pltpu.VMEM((2, quads, part, 4 * group), BF),
            pltpu.VMEM((2, max(quads - 1, 1), part, 4 * group), BF),
            pltpu.VMEM((2, part, 4 * group), BF),
            pltpu.VMEM((2, part, 4 * group), BF),
            pltpu.VMEM((2, quads, part, 4 * group), BF),
            pltpu.VMEM((2, group * 12, 128), F32),
            pltpu.VMEM((2, max(planes - 1, 1), 24, 128), F32),
            pltpu.VMEM((2, 2, 16, 128), F32),
            pltpu.VMEM((2, 3, 16, 128), F32),
            pltpu.VMEM((2, rows // 2, 4 * group), BF),
            pltpu.VMEM((nt - 1, rows // 2, 4 * group), BF),
            pltpu.VMEM((nt, rows // 2, 4 * group), BF),
            pltpu.SemaphoreType.DMA((11,)),
            pltpu.SemaphoreType.DMA((21,)),
            pltpu.SemaphoreType.DMA((21,)),
        ],
        compiler_params=pltpu.CompilerParams(
            collective_id=0, has_side_effects=True, vmem_limit_bytes=63 * 1024 * 1024
        ),
        cost_estimate=pl.CostEstimate(flops=600_000_000, bytes_accessed=5_000_000, transcendentals=0),
    )(x, cot.reshape(tokens * 2, 128), frz, dec, em, xm, emo, esq, xmo, xsq)
    factors = [em, xm, em, em, xm, xm]
    out = pl.pallas_call(
        spread,
        out_shape=(like(proj),) + tuple(like(f) for f in factors),
        in_specs=[vmem] * 2,
        out_specs=[hbm] * 7,
        scratch_shapes=[held(f) for f in factors] + [pltpu.SemaphoreType.DMA((7,))],
        cost_estimate=pl.CostEstimate(flops=10_000, bytes_accessed=60_000, transcendentals=0),
    )(new, proj)
    return (out[0].reshape(rows, 2, 128),) + tuple(out[1:])


def solution(mesh):
    nt = mesh.shape["tensor"]
    planes = mesh.shape["dp"] // QUAD
    ny = min(planes, 4)
    nx = planes // ny
    factor = P(None, "dp", "tensor")
    return jax.shard_map(
        functools.partial(body, nx, ny, nt),
        mesh=mesh,
        in_specs=(
            P("dp", "tensor"),
            P("dp", None, "tensor"),
            P(None, None, "tensor"),
            P("dp", None),
        )
        + (factor,) * 6,
        out_specs=(P("dp", None, "tensor"),) + (factor,) * 6,
        check_vma=False,
    )
```

```python
import functools

import jax
import jax.numpy as jnp
from jax import lax
from jax.experimental import pallas as pl
from jax.experimental.pallas import tpu as pltpu
from jax.sharding import PartitionSpec as P

adapter_scale_factor = 2.0
beta_first = 0.9
beta_second = 0.999
correct_first = 1.0 - 0.9**10
correct_second = 1.0 - 0.999**10
learn_rate = 0.002
decay_rate = 0.01
epsilon = 1e-08

BF = jnp.bfloat16
F32 = jnp.float32
QUAD = 4


def adam_step(master, moment, square, grad):
    moment_new = beta_first * moment + (1.0 - beta_first) * grad
    square_new = beta_second * square + (1.0 - beta_second) * grad * grad
    update = moment_new / correct_first / (jnp.sqrt(square_new / correct_second) + epsilon)
    return (master - learn_rate * (update + decay_rate * master), moment_new, square_new)


def dot(a, b, ca, cb):
    return lax.dot_general(a, b, (((ca,), (cb,)), ((), ())), preferred_element_type=F32)


def kernel(
    nx, ny, nt,
    x_hbm, cot_hbm, frz_hbm, dec_hbm, em_hbm, xm_hbm, emo_hbm, esq_hbm, xmo_hbm, xsq_hbm,
    proj_o, new_o,
    em, xm, emo, xmo, esq, xsq, xc, cot_v, frz_v, dec_v, dec2, wide, base,
    pack, ga, gb, fac, enew, xnew, lbf, lbs, l1, l2s, l2, lfull,
    gr, r1, rs, r2, zs, zl, zx,
    local_sem, send_sem, recv_sem,
):
    planes = nx * ny
    group = planes * 2
    quads = nt // 2
    tokens = xc.shape[0]
    feats = em_hbm.shape[2]
    me = lax.axis_index("dp")
    t = lax.axis_index("tensor")
    xy = lax.div(me, QUAD)
    q = lax.rem(me, QUAD)
    xi, yi = lax.div(xy, ny), lax.rem(xy, ny)
    zh, co = lax.div(q, 2), lax.rem(q, 2)
    tq, ti = lax.div(t, quads), lax.rem(t, quads)
    s = xy * 2 + co

    def plane_peer(k):
        return lax.rem(xi + k // ny, nx) * ny + lax.rem(yi + k % ny, ny)

    def device(pp, z, c):
        return pp * QUAD + z * 2 + c

    other_zh, other_co = 1 - zh, 1 - co
    order = sorted(
        range(1, planes), key=lambda k: -(min(k // ny, nx - k // ny) + min(k % ny, ny - k % ny))
    )
    plane = [(k, plane_peer(k)) for k in order]
    near = [device(pp, zh, c) for _, pp in plane for c in (co, other_co)]
    near.append(device(xy, zh, other_co))
    partner = device(xy, other_zh, co)
    cross = device(xy, other_zh, other_co)
    ring = sorted(range(1, nt), key=lambda k: abs(k - nt // 2))
    tens = [(k, lax.rem(t + k, nt)) for k in ring]
    far = [0] + ring[::-1]
    quad = [(k, tq * quads + lax.rem(ti + k, quads)) for k in range(1, quads)]
    opposite = (1 - tq) * quads + ti

    def send(stage, src, dst, dp, tn):
        pltpu.make_async_remote_copy(
            src_ref=src, dst_ref=dst, send_sem=send_sem.at[stage], recv_sem=recv_sem.at[stage],
            device_id=(dp, tn), device_id_type=pl.DeviceIdType.MESH,
        ).start()

    def descriptor(stage, ref):
        return pltpu.make_async_remote_copy(
            src_ref=ref, dst_ref=ref, send_sem=send_sem.at[stage], recv_sem=recv_sem.at[stage],
            device_id=(partner, t), device_id_type=pl.DeviceIdType.MESH,
        )

    sent = []

    def arrive(stage, ref):
        descriptor(stage, ref).wait_recv()
        sent.append((stage, ref))

    barrier = pltpu.get_barrier_semaphore()
    peers = [(partner, t), (cross, t)] + [(dp, t) for dp in near]
    peers += [(dp, tt) for _, tt in tens for dp in (me, partner)]
    for peer in peers:
        pl.semaphore_signal(barrier, inc=1, device_id=peer, device_id_type=pl.DeviceIdType.MESH)

    here = pl.ds(pl.multiple_of(t * feats, feats), feats)
    loads = [
        pltpu.make_async_copy(src, dst, local_sem.at[i])
        for i, (src, dst) in enumerate(
            (
                (em_hbm, em),
                (xm_hbm, xm),
                (emo_hbm, emo),
                (xmo_hbm, xmo),
                (esq_hbm, esq),
                (xsq_hbm, xsq),
                (cot_hbm, cot_v),
                (x_hbm, xc.at[:, pl.ds(0, feats)]),
                (dec_hbm.at[:, here], dec2.at[0]),
                (dec_hbm, dec_v),
                (frz_hbm, frz_v),
            )
        )
    ]
    for load in loads:
        load.start()

    pack[0] = jnp.zeros(pack.shape[1:], F32)
    for i, (e_ref, o_ref) in enumerate(((em, xm), (emo, xmo), (esq, xsq))):
        loads[2 * i].wait()
        loads[2 * i + 1].wait()
        for p in range(2):
            for c in range(5):
                pack[0, i, p * 6 + c : p * 6 + c + 1, :] = e_ref[p, :, c * 128 : (c + 1) * 128]
            pack[0, i, p * 6 + 5 : p * 6 + 6, :] = o_ref[p, :, :]
    ga[0, s] = pack[0, 0].astype(BF)
    fac[...] = jnp.zeros_like(fac)
    xnew[...] = jnp.zeros_like(xnew)
    rs[...] = jnp.zeros_like(rs)
    loads[6].wait()
    wide[0 : 2 * tokens, :] = cot_v[...].astype(F32)
    for p in range(2):
        xc[:, feats + p * 128 : feats + (p + 1) * 128] = wide[pl.ds(p, tokens, stride=2), :].astype(BF)
    loads[7].wait()
    loads[8].wait()

    pl.semaphore_wait(barrier, len(peers))

    def spread_rows(stage, rows):
        for dp in near:
            send(stage, rows, rows, dp, t)

    send(1, ga.at[0, s], ga.at[1, s], partner, t)
    spread_rows(0, ga.at[0, s])
    send(17, pack.at[0], pack.at[1], partner, t)
    half_rows = dec_v.shape[0] // 2

    def send_decode(first, count):
        these = pl.ds(first, count)
        send(18, dec2.at[0, these], dec2.at[1, these], partner, t)

    send_decode(0, half_rows)

    def project(half):
        wide[0 : group * 16, :] = ga[half].reshape(group * 16, 128).astype(F32)
        for p in range(2):
            for c in range(6):
                piece = wide[pl.ds(p * 6 + c, group, stride=16), :].astype(BF)
                if c < 5:
                    fac[half, p * group : (p + 1) * group, c * 128 : (c + 1) * 128] = piece
                else:
                    rows = slice((2 + p) * group, (3 + p) * group)
                    fac[half, rows, feats + p * 128 : feats + (p + 1) * 128] = piece
        lbf[half] = dot(xc[...], fac[half], 1, 1)
        lbs[half] = lbf[half].astype(BF).reshape(lbs.shape[1:])
        for k, tt in quad:
            send(3 + half, lbs.at[half, lax.rem(tt, quads)], l1.at[half, k - 1], me, tt)

    part = tokens // quads

    def sum_quad(half):
        if quads > 1:
            arrive(3 + half, l1.at[half])
        total = lbf[half, pl.ds(pl.multiple_of(ti * part, part), part), :]
        for k in range(quads - 1):
            total = total + l1[half, k].astype(F32)
        lbf[half, 0:part, :] = total
        l2s[half] = total.astype(BF)
        send(5 + half, l2s.at[half], l2.at[half], me, opposite)

    def sum_all(half):
        arrive(5 + half, l2.at[half])
        lfull[half, ti] = (lbf[half, 0:part, :] + l2[half].astype(F32)).astype(BF)
        for k, tt in quad:
            send(7 + half, lfull.at[half, ti], lfull.at[half, ti], me, tt)

    def gradients(half):
        if quads > 1:
            arrive(7 + half, lfull.at[half, pl.ds(0, quads - 1)])
        if half == 1:
            send_decode(half_rows, half_rows)
        both = lfull[half].reshape(tokens, 4 * group)
        g = adapter_scale_factor * dot(both, xc[...], 0, 0)
        for p in range(2):
            for c in range(5):
                gr[half, pl.ds(p * 6 + c, group, stride=12), :] = g[
                    (2 + p) * group : (3 + p) * group, c * 128 : (c + 1) * 128
                ]
            gr[half, pl.ds(p * 6 + 5, group, stride=12), :] = g[
                p * group : (p + 1) * group, feats + p * 128 : feats + (p + 1) * 128
            ]
        for k, pp in plane:
            src = gr.at[half, pl.ds(pl.multiple_of(pp * 24, 24), 24)]
            send(9 + half, src, r1.at[half, k - 1], device(pp, zh, co), t)

    def sum_plane(half):
        if planes > 1:
            arrive(9 + half, r1.at[half])
        total = gr[half, pl.ds(pl.multiple_of(xy * 24, 24), 24), :]
        for k in range(planes - 1):
            total = total + r1[half, k]
        for c in range(2):
            rs[half, c, :12, :] = total[c * 12 : (c + 1) * 12, :]
        send(11 + half, rs.at[half, other_co], r2.at[half, 0], device(xy, zh, other_co), t)
        send(14 - half, rs.at[half, co], r2.at[1 - half, 1], partner, t)
        send(14 - half, rs.at[half, other_co], r2.at[1 - half, 2], cross, t)

    arrive(0, ga.at[0, pl.ds(0, group - 1)])
    project(0)
    arrive(1, ga.at[1, s])
    spread_rows(2, ga.at[1, s])
    sum_quad(0)
    arrive(2, ga.at[1, pl.ds(0, group - 1)])
    project(1)
    sum_all(0)
    sum_quad(1)
    gradients(0)
    sum_all(1)
    sum_plane(0)
    gradients(1)
    loads[9].wait()
    loads[10].wait()
    for p in range(2):
        base[:, p * 128 : (p + 1) * 128] = dot(dec_v[...], frz_v[p], 1, 0)

    sum_plane(1)

    def update(half):
        arrive(11 + half, r2.at[half, 0])
        arrive(13 + half, r2.at[half, pl.ds(1, 2)])
        grad = (rs[half, co] + r2[half, 0]) + (r2[half, 1] + r2[half, 2])
        return adam_step(pack[half, 0], pack[half, 1], pack[half, 2], grad)

    def unpack_new(half, pieces):
        wide[0 : group * 16, :] = gb[half].reshape(group * 16, 128).astype(F32)
        for p in range(2):
            for c in pieces:
                piece = wide[pl.ds(p * 6 + c, group, stride=16), :].astype(BF)
                if c < 5:
                    enew[p * group : (p + 1) * group, c * 128 : (c + 1) * 128] = piece
                else:
                    rows = slice((half * 2 + p) * group, (half * 2 + p + 1) * group)
                    xnew[rows, p * 128 : (p + 1) * 128] = piece

    arrive(17, pack.at[1])
    gb[1, s] = update(1)[0].astype(BF)
    spread_rows(15, gb.at[1, s])
    arrive(18, dec2.at[1])
    arrive(15, gb.at[1, pl.ds(0, group - 1)])
    unpack_new(1, range(5))
    inner = []
    for i in (1, 0):
        v = adapter_scale_factor * dot(dec2[i], enew[...], 1, 1)
        inner.append(jnp.concatenate([v[:half_rows], v[half_rows:]], axis=1))
        zs[1 - i] = inner[-1].astype(BF)
        if i == 1:
            for k in far:
                send(20, zs.at[0], zx.at[k], partner, lax.rem(t + k, nt))
    for k, tt in tens:
        send(16, zs.at[1], zl.at[k - 1], me, tt)
    unpack_new(1, (5,))

    after, moment, square = update(0)
    gb[0, s] = after.astype(BF)
    spread_rows(19, gb.at[0, s])
    for i, value in enumerate((after, moment, square)):
        new_o[i] = value
    arrive(19, gb.at[0, pl.ds(0, group - 1)])
    unpack_new(0, (5,))

    arrive(16, zl)
    arrive(20, zx)
    own, other = zx[0].astype(F32), inner[1]
    for k in range(nt - 1):
        own = own + zx[k + 1].astype(F32)
        other = other + zl[k].astype(F32)
    both = jnp.concatenate(
        [
            jnp.concatenate([v[:, : 2 * group], v[:, 2 * group :]], axis=0)
            for v in (own.astype(BF), other.astype(BF))
        ],
        axis=1,
    )
    out = base[...] + dot(both, xnew[...], 1, 0)
    rows = 2 * half_rows
    for p in range(2):
        wide[pl.ds(p, rows, stride=2), :] = out[:, p * 128 : (p + 1) * 128]
    proj_o[...] = wide[0 : 2 * rows, :].astype(BF)

    for stage, ref in sent:
        descriptor(stage, ref).wait_send()


def spread(new, proj, *rest):
    outs, parts, sem = rest[:7], rest[7:13], rest[13]
    copies = [pltpu.make_async_copy(proj, outs[0], sem.at[0])]
    copies[0].start()
    for i, (e, o) in enumerate(((0, 1), (2, 4), (3, 5))):
        for p in range(2):
            for c in range(5):
                row = p * 6 + c
                parts[e][p, :, c * 128 : (c + 1) * 128] = new[i, row : row + 1, :]
            parts[o][p, :, :] = new[i, p * 6 + 5 : p * 6 + 6, :]
        for n in (e, o):
            copies.append(pltpu.make_async_copy(parts[n], outs[n + 1], sem.at[n + 1]))
            copies[-1].start()
    for copy in copies:
        copy.wait()


def body(nx, ny, nt, x, cot, frz, dec, em, xm, emo, esq, xmo, xsq):
    tokens, feats = x.shape
    rows = dec.shape[0]
    planes = nx * ny
    group = planes * 2
    quads = nt // 2
    part = tokens // quads
    hbm = pl.BlockSpec(memory_space=pltpu.HBM)
    vmem = pl.BlockSpec(memory_space=pltpu.VMEM)
    like = lambda a: jax.ShapeDtypeStruct(a.shape, a.dtype)
    held = lambda a: pltpu.VMEM(a.shape, a.dtype)
    proj, new = pl.pallas_call(
        functools.partial(kernel, nx, ny, nt),
        out_shape=(
            jax.ShapeDtypeStruct((rows * 2, 128), BF),
            jax.ShapeDtypeStruct((3, 16, 128), F32),
        ),
        in_specs=[hbm] * 10,
        out_specs=[vmem] * 2,
        scratch_shapes=[
            held(em), held(xm), held(em), held(xm), held(em), held(xm),
            pltpu.VMEM((tokens, feats + 256), BF),
            pltpu.VMEM((tokens * 2, 128), BF),
            held(frz),
            held(dec),
            pltpu.VMEM((2, rows, feats), BF),
            pltpu.VMEM((max(2 * tokens, group * 16) + 16, 128), F32),
            pltpu.VMEM((rows, 256), F32),
            pltpu.VMEM((2, 3, 16, 128), F32),
            pltpu.VMEM((2, group, 16, 128), BF),
            pltpu.VMEM((2, group, 16, 128), BF),
            pltpu.VMEM((2, 4 * group, feats + 256), BF),
            pltpu.VMEM((2 * group, feats), BF),
            pltpu.VMEM((4 * group, 256), BF),
            pltpu.VMEM((2, tokens, 4 * group), F32),
            pltpu.VMEM((2, quads, part, 4 * group), BF),
            pltpu.VMEM((2, max(quads - 1, 1), part, 4 * group), BF),
            pltpu.VMEM((2, part, 4 * group), BF),
            pltpu.VMEM((2, part, 4 * group), BF),
            pltpu.VMEM((2, quads, part, 4 * group), BF),
            pltpu.VMEM((2, group * 12 + 16, 128), F32),
            pltpu.VMEM((2, max(planes - 1, 1), 24, 128), F32),
            pltpu.VMEM((2, 2, 16, 128), F32),
            pltpu.VMEM((2, 3, 16, 128), F32),
            pltpu.VMEM((2, rows // 2, 4 * group), BF),
            pltpu.VMEM((nt - 1, rows // 2, 4 * group), BF),
            pltpu.VMEM((nt, rows // 2, 4 * group), BF),
            pltpu.SemaphoreType.DMA((11,)),
            pltpu.SemaphoreType.DMA((21,)),
            pltpu.SemaphoreType.DMA((21,)),
        ],
        compiler_params=pltpu.CompilerParams(
            collective_id=0, has_side_effects=True, vmem_limit_bytes=63 * 1024 * 1024
        ),
        cost_estimate=pl.CostEstimate(flops=600_000_000, bytes_accessed=5_000_000, transcendentals=0),
    )(x, cot.reshape(tokens * 2, 128), frz, dec, em, xm, emo, esq, xmo, xsq)
    factors = [em, xm, em, em, xm, xm]
    out = pl.pallas_call(
        spread,
        out_shape=(like(proj),) + tuple(like(f) for f in factors),
        in_specs=[vmem] * 2,
        out_specs=[hbm] * 7,
        scratch_shapes=[held(f) for f in factors] + [pltpu.SemaphoreType.DMA((7,))],
        cost_estimate=pl.CostEstimate(flops=10_000, bytes_accessed=60_000, transcendentals=0),
    )(new, proj)
    return (out[0].reshape(rows, 2, 128),) + tuple(out[1:])


def solution(mesh):
    nt = mesh.shape["tensor"]
    planes = mesh.shape["dp"] // QUAD
    ny = min(planes, 4)
    nx = planes // ny
    factor = P(None, "dp", "tensor")
    return jax.shard_map(
        functools.partial(body, nx, ny, nt),
        mesh=mesh,
        in_specs=(
            P("dp", "tensor"),
            P("dp", None, "tensor"),
            P(None, None, "tensor"),
            P("dp", None),
        )
        + (factor,) * 6,
        out_specs=(P("dp", None, "tensor"),) + (factor,) * 6,
        check_vma=False,
    )
```

```python
import functools

import jax
import jax.numpy as jnp
from jax import lax
from jax.experimental import pallas as pl
from jax.experimental.pallas import tpu as pltpu
from jax.sharding import PartitionSpec as P

adapter_scale_factor = 2.0
beta_first = 0.9
beta_second = 0.999
correct_first = 1.0 - 0.9**10
correct_second = 1.0 - 0.999**10
learn_rate = 0.002
decay_rate = 0.01
epsilon = 1e-08

BF = jnp.bfloat16
F32 = jnp.float32
QUAD = 4


def adam_step(master, moment, square, grad):
    moment_new = beta_first * moment + (1.0 - beta_first) * grad
    square_new = beta_second * square + (1.0 - beta_second) * grad * grad
    update = moment_new / correct_first / (jnp.sqrt(square_new / correct_second) + epsilon)
    return (master - learn_rate * (update + decay_rate * master), moment_new, square_new)


def dot(a, b, ca, cb):
    return lax.dot_general(a, b, (((ca,), (cb,)), ((), ())), preferred_element_type=F32)


def kernel(
    nx, ny, nt,
    x_hbm, cot_hbm, frz_hbm, dec_hbm, em_hbm, xm_hbm, emo_hbm, esq_hbm, xmo_hbm, xsq_hbm,
    proj_o, new_o,
    em, xm, emo, xmo, esq, xsq, xc, cot_v, frz_v, dec_v, dec2, wide, base,
    pack, ga, gb, fac, enew, xnew, lbf, lbs, l1, l2s, l2, lfull,
    gr, grb, r1, rs, r2, zs, zl, zx,
    local_sem, send_sem, recv_sem,
):
    planes = nx * ny
    group = planes * 2
    quads = nt // 2
    tokens = xc.shape[0]
    feats = em_hbm.shape[2]
    me = lax.axis_index("dp")
    t = lax.axis_index("tensor")
    xy = lax.div(me, QUAD)
    q = lax.rem(me, QUAD)
    xi, yi = lax.div(xy, ny), lax.rem(xy, ny)
    zh, co = lax.div(q, 2), lax.rem(q, 2)
    tq, ti = lax.div(t, quads), lax.rem(t, quads)
    s = xy * 2 + co

    def plane_peer(k):
        return lax.rem(xi + k // ny, nx) * ny + lax.rem(yi + k % ny, ny)

    def device(pp, z, c):
        return pp * QUAD + z * 2 + c

    other_zh, other_co = 1 - zh, 1 - co
    order = sorted(
        range(1, planes), key=lambda k: -(min(k // ny, nx - k // ny) + min(k % ny, ny - k % ny))
    )
    plane = [(k, plane_peer(k)) for k in order]
    near = [device(pp, zh, c) for _, pp in plane for c in (co, other_co)]
    near.append(device(xy, zh, other_co))
    partner = device(xy, other_zh, co)
    cross = device(xy, other_zh, other_co)
    ring = sorted(range(1, nt), key=lambda k: abs(k - nt // 2))
    tens = [(k, lax.rem(t + k, nt)) for k in ring]
    far = [0] + ring[::-1]
    quad = [(k, tq * quads + lax.rem(ti + k, quads)) for k in range(1, quads)]
    opposite = (1 - tq) * quads + ti

    def send(stage, src, dst, dp, tn):
        pltpu.make_async_remote_copy(
            src_ref=src, dst_ref=dst, send_sem=send_sem.at[stage], recv_sem=recv_sem.at[stage],
            device_id=(dp, tn), device_id_type=pl.DeviceIdType.MESH,
        ).start()

    def descriptor(stage, ref):
        return pltpu.make_async_remote_copy(
            src_ref=ref, dst_ref=ref, send_sem=send_sem.at[stage], recv_sem=recv_sem.at[stage],
            device_id=(partner, t), device_id_type=pl.DeviceIdType.MESH,
        )

    sent = []

    def arrive(stage, ref):
        descriptor(stage, ref).wait_recv()
        sent.append((stage, ref))

    barrier = pltpu.get_barrier_semaphore()
    peers = [(partner, t), (cross, t)] + [(dp, t) for dp in near]
    peers += [(dp, tt) for _, tt in tens for dp in (me, partner)]
    for peer in peers:
        pl.semaphore_signal(barrier, inc=1, device_id=peer, device_id_type=pl.DeviceIdType.MESH)

    here = pl.ds(pl.multiple_of(t * feats, feats), feats)
    loads = [
        pltpu.make_async_copy(src, dst, local_sem.at[i])
        for i, (src, dst) in enumerate(
            (
                (em_hbm, em),
                (xm_hbm, xm),
                (emo_hbm, emo),
                (xmo_hbm, xmo),
                (esq_hbm, esq),
                (xsq_hbm, xsq),
                (cot_hbm, cot_v),
                (x_hbm, xc.at[:, pl.ds(0, feats)]),
                (dec_hbm.at[:, here], dec2.at[0]),
                (dec_hbm, dec_v),
                (frz_hbm, frz_v),
            )
        )
    ]
    for load in loads:
        load.start()

    pack[0] = jnp.zeros(pack.shape[1:], F32)
    for i, (e_ref, o_ref) in enumerate(((em, xm), (emo, xmo), (esq, xsq))):
        loads[2 * i].wait()
        loads[2 * i + 1].wait()
        for p in range(2):
            for c in range(5):
                pack[0, i, p * 6 + c : p * 6 + c + 1, :] = e_ref[p, :, c * 128 : (c + 1) * 128]
            pack[0, i, p * 6 + 5 : p * 6 + 6, :] = o_ref[p, :, :]
    ga[0, s] = pack[0, 0].astype(BF)
    fac[...] = jnp.zeros_like(fac)
    xnew[...] = jnp.zeros_like(xnew)
    rs[...] = jnp.zeros_like(rs)
    grb[...] = jnp.zeros_like(grb)
    loads[6].wait()
    wide[0 : 2 * tokens, :] = cot_v[...].astype(F32)
    for p in range(2):
        xc[:, feats + p * 128 : feats + (p + 1) * 128] = wide[pl.ds(p, tokens, stride=2), :].astype(BF)
    loads[7].wait()
    loads[8].wait()

    pl.semaphore_wait(barrier, len(peers))

    def spread_rows(stage, rows):
        for dp in near:
            send(stage, rows, rows, dp, t)

    send(1, ga.at[0, s], ga.at[1, s], partner, t)
    spread_rows(0, ga.at[0, s])
    send(17, pack.at[0], pack.at[1], partner, t)
    half_rows = dec_v.shape[0] // 2

    def send_decode(first, count):
        these = pl.ds(first, count)
        send(18, dec2.at[0, these], dec2.at[1, these], partner, t)

    send_decode(0, half_rows)

    def project(half):
        wide[0 : group * 16, :] = ga[half].reshape(group * 16, 128).astype(F32)
        for p in range(2):
            for c in range(6):
                piece = wide[pl.ds(p * 6 + c, group, stride=16), :].astype(BF)
                if c < 5:
                    fac[half, p * group : (p + 1) * group, c * 128 : (c + 1) * 128] = piece
                else:
                    rows = slice((2 + p) * group, (3 + p) * group)
                    fac[half, rows, feats + p * 128 : feats + (p + 1) * 128] = piece
        lbf[half] = dot(xc[...], fac[half], 1, 1)
        lbs[half] = lbf[half].astype(BF).reshape(lbs.shape[1:])
        for k, tt in quad:
            send(3 + half, lbs.at[half, lax.rem(tt, quads)], l1.at[half, k - 1], me, tt)

    part = tokens // quads

    def sum_quad(half):
        if quads > 1:
            arrive(3 + half, l1.at[half])
        total = lbf[half, pl.ds(pl.multiple_of(ti * part, part), part), :]
        for k in range(quads - 1):
            total = total + l1[half, k].astype(F32)
        lbf[half, 0:part, :] = total
        l2s[half] = total.astype(BF)
        send(5 + half, l2s.at[half], l2.at[half], me, opposite)

    def sum_all(half):
        arrive(5 + half, l2.at[half])
        lfull[half, ti] = (lbf[half, 0:part, :] + l2[half].astype(F32)).astype(BF)
        for k, tt in quad:
            send(7 + half, lfull.at[half, ti], lfull.at[half, ti], me, tt)

    def gradients(half):
        if quads > 1:
            arrive(7 + half, lfull.at[half, pl.ds(0, quads - 1)])
        if half == 1:
            send_decode(half_rows, half_rows)
        both = lfull[half].reshape(tokens, 4 * group)
        g = adapter_scale_factor * dot(both, xc[...], 0, 0)
        for p in range(2):
            for c in range(5):
                gr[half, pl.ds(p * 6 + c, group, stride=12), :] = g[
                    (2 + p) * group : (3 + p) * group, c * 128 : (c + 1) * 128
                ]
            gr[half, pl.ds(p * 6 + 5, group, stride=12), :] = g[
                p * group : (p + 1) * group, feats + p * 128 : feats + (p + 1) * 128
            ]
        sums = gr[half, 0 : group * 12, :].reshape(planes, 24, 128)
        grb[half, :, :24, :] = sums.astype(BF)
        for k, pp in plane:
            send(9 + half, grb.at[half, pp], r1.at[half, k - 1], device(pp, zh, co), t)

    def sum_plane(half):
        if planes > 1:
            arrive(9 + half, r1.at[half])
        total = gr[half, pl.ds(pl.multiple_of(xy * 24, 24), 24), :]
        for k in range(planes - 1):
            total = total + r1[half, k].astype(F32)[:24]
        for c in range(2):
            rs[half, c, :12, :] = total[c * 12 : (c + 1) * 12, :]
        send(11 + half, rs.at[half, other_co], r2.at[half, 0], device(xy, zh, other_co), t)
        send(14 - half, rs.at[half, co], r2.at[1 - half, 1], partner, t)
        send(14 - half, rs.at[half, other_co], r2.at[1 - half, 2], cross, t)

    arrive(0, ga.at[0, pl.ds(0, group - 1)])
    project(0)
    arrive(1, ga.at[1, s])
    spread_rows(2, ga.at[1, s])
    sum_quad(0)
    arrive(2, ga.at[1, pl.ds(0, group - 1)])
    project(1)
    sum_all(0)
    sum_quad(1)
    gradients(0)
    sum_all(1)
    sum_plane(0)
    gradients(1)
    loads[9].wait()
    loads[10].wait()
    for p in range(2):
        base[:, p * 128 : (p + 1) * 128] = dot(dec_v[...], frz_v[p], 1, 0)

    sum_plane(1)

    def update(half):
        arrive(11 + half, r2.at[half, 0])
        arrive(13 + half, r2.at[half, pl.ds(1, 2)])
        grad = (rs[half, co] + r2[half, 0]) + (r2[half, 1] + r2[half, 2])
        return adam_step(pack[half, 0], pack[half, 1], pack[half, 2], grad)

    def unpack_new(half, pieces):
        wide[0 : group * 16, :] = gb[half].reshape(group * 16, 128).astype(F32)
        for p in range(2):
            for c in pieces:
                piece = wide[pl.ds(p * 6 + c, group, stride=16), :].astype(BF)
                if c < 5:
                    enew[p * group : (p + 1) * group, c * 128 : (c + 1) * 128] = piece
                else:
                    rows = slice((half * 2 + p) * group, (half * 2 + p + 1) * group)
                    xnew[rows, p * 128 : (p + 1) * 128] = piece

    arrive(17, pack.at[1])
    gb[1, s] = update(1)[0].astype(BF)
    spread_rows(15, gb.at[1, s])
    arrive(18, dec2.at[1])
    arrive(15, gb.at[1, pl.ds(0, group - 1)])
    unpack_new(1, range(5))
    inner = []
    for i in (1, 0):
        v = adapter_scale_factor * dot(dec2[i], enew[...], 1, 1)
        inner.append(jnp.concatenate([v[:half_rows], v[half_rows:]], axis=1))
        zs[1 - i] = inner[-1].astype(BF)
        if i == 1:
            for k in far:
                send(20, zs.at[0], zx.at[k], partner, lax.rem(t + k, nt))
    for k, tt in tens:
        send(16, zs.at[1], zl.at[k - 1], me, tt)
    unpack_new(1, (5,))

    after, moment, square = update(0)
    gb[0, s] = after.astype(BF)
    spread_rows(19, gb.at[0, s])
    for i, value in enumerate((after, moment, square)):
        new_o[i] = value
    arrive(19, gb.at[0, pl.ds(0, group - 1)])
    unpack_new(0, (5,))

    arrive(16, zl)
    arrive(20, zx)
    own, other = zx[0].astype(F32), inner[1]
    for k in range(nt - 1):
        own = own + zx[k + 1].astype(F32)
        other = other + zl[k].astype(F32)
    both = jnp.concatenate(
        [
            jnp.concatenate([v[:, : 2 * group], v[:, 2 * group :]], axis=0)
            for v in (own.astype(BF), other.astype(BF))
        ],
        axis=1,
    )
    out = base[...] + dot(both, xnew[...], 1, 0)
    rows = 2 * half_rows
    for p in range(2):
        wide[pl.ds(p, rows, stride=2), :] = out[:, p * 128 : (p + 1) * 128]
    proj_o[...] = wide[0 : 2 * rows, :].astype(BF)

    for stage, ref in sent:
        descriptor(stage, ref).wait_send()


def spread(new, proj, *rest):
    outs, parts, sem = rest[:7], rest[7:13], rest[13]
    copies = [pltpu.make_async_copy(proj, outs[0], sem.at[0])]
    copies[0].start()
    for i, (e, o) in enumerate(((0, 1), (2, 4), (3, 5))):
        for p in range(2):
            for c in range(5):
                row = p * 6 + c
                parts[e][p, :, c * 128 : (c + 1) * 128] = new[i, row : row + 1, :]
            parts[o][p, :, :] = new[i, p * 6 + 5 : p * 6 + 6, :]
        for n in (e, o):
            copies.append(pltpu.make_async_copy(parts[n], outs[n + 1], sem.at[n + 1]))
            copies[-1].start()
    for copy in copies:
        copy.wait()


def body(nx, ny, nt, x, cot, frz, dec, em, xm, emo, esq, xmo, xsq):
    tokens, feats = x.shape
    rows = dec.shape[0]
    planes = nx * ny
    group = planes * 2
    quads = nt // 2
    part = tokens // quads
    hbm = pl.BlockSpec(memory_space=pltpu.HBM)
    vmem = pl.BlockSpec(memory_space=pltpu.VMEM)
    like = lambda a: jax.ShapeDtypeStruct(a.shape, a.dtype)
    held = lambda a: pltpu.VMEM(a.shape, a.dtype)
    proj, new = pl.pallas_call(
        functools.partial(kernel, nx, ny, nt),
        out_shape=(
            jax.ShapeDtypeStruct((rows * 2, 128), BF),
            jax.ShapeDtypeStruct((3, 16, 128), F32),
        ),
        in_specs=[hbm] * 10,
        out_specs=[vmem] * 2,
        scratch_shapes=[
            held(em), held(xm), held(em), held(xm), held(em), held(xm),
            pltpu.VMEM((tokens, feats + 256), BF),
            pltpu.VMEM((tokens * 2, 128), BF),
            held(frz),
            held(dec),
            pltpu.VMEM((2, rows, feats), BF),
            pltpu.VMEM((max(2 * tokens, group * 16) + 16, 128), F32),
            pltpu.VMEM((rows, 256), F32),
            pltpu.VMEM((2, 3, 16, 128), F32),
            pltpu.VMEM((2, group, 16, 128), BF),
            pltpu.VMEM((2, group, 16, 128), BF),
            pltpu.VMEM((2, 4 * group, feats + 256), BF),
            pltpu.VMEM((2 * group, feats), BF),
            pltpu.VMEM((4 * group, 256), BF),
            pltpu.VMEM((2, tokens, 4 * group), F32),
            pltpu.VMEM((2, quads, part, 4 * group), BF),
            pltpu.VMEM((2, max(quads - 1, 1), part, 4 * group), BF),
            pltpu.VMEM((2, part, 4 * group), BF),
            pltpu.VMEM((2, part, 4 * group), BF),
            pltpu.VMEM((2, quads, part, 4 * group), BF),
            pltpu.VMEM((2, group * 12 + 16, 128), F32),
            pltpu.VMEM((2, planes, 32, 128), BF),
            pltpu.VMEM((2, max(planes - 1, 1), 32, 128), BF),
            pltpu.VMEM((2, 2, 16, 128), F32),
            pltpu.VMEM((2, 3, 16, 128), F32),
            pltpu.VMEM((2, rows // 2, 4 * group), BF),
            pltpu.VMEM((nt - 1, rows // 2, 4 * group), BF),
            pltpu.VMEM((nt, rows // 2, 4 * group), BF),
            pltpu.SemaphoreType.DMA((11,)),
            pltpu.SemaphoreType.DMA((21,)),
            pltpu.SemaphoreType.DMA((21,)),
        ],
        compiler_params=pltpu.CompilerParams(
            collective_id=0, has_side_effects=True, vmem_limit_bytes=63 * 1024 * 1024
        ),
        cost_estimate=pl.CostEstimate(flops=600_000_000, bytes_accessed=5_000_000, transcendentals=0),
    )(x, cot.reshape(tokens * 2, 128), frz, dec, em, xm, emo, esq, xmo, xsq)
    factors = [em, xm, em, em, xm, xm]
    out = pl.pallas_call(
        spread,
        out_shape=(like(proj),) + tuple(like(f) for f in factors),
        in_specs=[vmem] * 2,
        out_specs=[hbm] * 7,
        scratch_shapes=[held(f) for f in factors] + [pltpu.SemaphoreType.DMA((7,))],
        cost_estimate=pl.CostEstimate(flops=10_000, bytes_accessed=60_000, transcendentals=0),
    )(new, proj)
    return (out[0].reshape(rows, 2, 128),) + tuple(out[1:])


def solution(mesh):
    nt = mesh.shape["tensor"]
    planes = mesh.shape["dp"] // QUAD
    ny = min(planes, 4)
    nx = planes // ny
    factor = P(None, "dp", "tensor")
    return jax.shard_map(
        functools.partial(body, nx, ny, nt),
        mesh=mesh,
        in_specs=(
            P("dp", "tensor"),
            P("dp", None, "tensor"),
            P(None, None, "tensor"),
            P("dp", None),
        )
        + (factor,) * 6,
        out_specs=(P("dp", None, "tensor"),) + (factor,) * 6,
        check_vma=False,
    )
```

```python
import functools

import jax
import jax.numpy as jnp
from jax import lax
from jax.experimental import pallas as pl
from jax.experimental.pallas import tpu as pltpu
from jax.sharding import PartitionSpec as P

adapter_scale_factor = 2.0
beta_first = 0.9
beta_second = 0.999
correct_first = 1.0 - 0.9**10
correct_second = 1.0 - 0.999**10
learn_rate = 0.002
decay_rate = 0.01
epsilon = 1e-08

BF = jnp.bfloat16
F32 = jnp.float32
QUAD = 4


def adam_step(master, moment, square, grad):
    moment_new = beta_first * moment + (1.0 - beta_first) * grad
    square_new = beta_second * square + (1.0 - beta_second) * grad * grad
    update = moment_new / correct_first / (jnp.sqrt(square_new / correct_second) + epsilon)
    return (master - learn_rate * (update + decay_rate * master), moment_new, square_new)


def dot(a, b, ca, cb):
    return lax.dot_general(a, b, (((ca,), (cb,)), ((), ())), preferred_element_type=F32)


def kernel(
    nx, ny, nt,
    x_hbm, cot_hbm, frz_hbm, dec_hbm, em_hbm, xm_hbm, emo_hbm, esq_hbm, xmo_hbm, xsq_hbm,
    proj_o, new_o,
    em, xm, emo, xmo, esq, xsq, xc, cot_v, frz_v, dec_v, dec2, wide, base,
    pack, ga, gb, fac, enew, xnew, lbf, lbs, l1, l2s, l2, lfull,
    gr, r1, rs, r2, zs, zl, zx,
    local_sem, send_sem, recv_sem,
):
    planes = nx * ny
    group = planes * 2
    quads = nt // 2
    tokens = xc.shape[0]
    feats = em_hbm.shape[2]
    me = lax.axis_index("dp")
    t = lax.axis_index("tensor")
    xy = lax.div(me, QUAD)
    q = lax.rem(me, QUAD)
    xi, yi = lax.div(xy, ny), lax.rem(xy, ny)
    zh, co = lax.div(q, 2), lax.rem(q, 2)
    tq, ti = lax.div(t, quads), lax.rem(t, quads)
    s = xy * 2 + co

    def plane_peer(k):
        return lax.rem(xi + k // ny, nx) * ny + lax.rem(yi + k % ny, ny)

    def device(pp, z, c):
        return pp * QUAD + z * 2 + c

    other_zh, other_co = 1 - zh, 1 - co
    order = sorted(
        range(1, planes), key=lambda k: -(min(k // ny, nx - k // ny) + min(k % ny, ny - k % ny))
    )
    plane = [(k, plane_peer(k)) for k in order]
    near = [device(pp, zh, c) for _, pp in plane for c in (co, other_co)]
    near.append(device(xy, zh, other_co))
    partner = device(xy, other_zh, co)
    cross = device(xy, other_zh, other_co)
    ring = sorted(range(1, nt), key=lambda k: abs(k - nt // 2))
    tens = [(k, lax.rem(t + k, nt)) for k in ring]
    far = [0] + ring[::-1]
    quad = [(k, tq * quads + lax.rem(ti + k, quads)) for k in range(1, quads)]
    opposite = (1 - tq) * quads + ti

    def send(stage, src, dst, dp, tn):
        pltpu.make_async_remote_copy(
            src_ref=src, dst_ref=dst, send_sem=send_sem.at[stage], recv_sem=recv_sem.at[stage],
            device_id=(dp, tn), device_id_type=pl.DeviceIdType.MESH,
        ).start()

    def descriptor(stage, ref):
        return pltpu.make_async_remote_copy(
            src_ref=ref, dst_ref=ref, send_sem=send_sem.at[stage], recv_sem=recv_sem.at[stage],
            device_id=(partner, t), device_id_type=pl.DeviceIdType.MESH,
        )

    sent = []

    def arrive(stage, ref):
        descriptor(stage, ref).wait_recv()
        sent.append((stage, ref))

    barrier = pltpu.get_barrier_semaphore()
    peers = [(partner, t), (cross, t)] + [(dp, t) for dp in near]
    peers += [(dp, tt) for _, tt in tens for dp in (me, partner)]
    for peer in peers:
        pl.semaphore_signal(barrier, inc=1, device_id=peer, device_id_type=pl.DeviceIdType.MESH)

    here = pl.ds(pl.multiple_of(t * feats, feats), feats)
    loads = [
        pltpu.make_async_copy(src, dst, local_sem.at[i])
        for i, (src, dst) in enumerate(
            (
                (em_hbm, em),
                (xm_hbm, xm),
                (emo_hbm, emo),
                (xmo_hbm, xmo),
                (esq_hbm, esq),
                (xsq_hbm, xsq),
                (cot_hbm, cot_v),
                (x_hbm, xc.at[:, pl.ds(0, feats)]),
                (dec_hbm.at[:, here], dec2.at[0]),
                (dec_hbm, dec_v),
                (frz_hbm, frz_v),
            )
        )
    ]
    for load in loads:
        load.start()

    pack[0] = jnp.zeros(pack.shape[1:], F32)
    for i, (e_ref, o_ref) in enumerate(((em, xm), (emo, xmo), (esq, xsq))):
        loads[2 * i].wait()
        loads[2 * i + 1].wait()
        for p in range(2):
            for c in range(5):
                pack[0, i, p * 6 + c : p * 6 + c + 1, :] = e_ref[p, :, c * 128 : (c + 1) * 128]
            pack[0, i, p * 6 + 5 : p * 6 + 6, :] = o_ref[p, :, :]
    ga[0, s] = pack[0, 0].astype(BF)
    fac[...] = jnp.zeros_like(fac)
    xnew[...] = jnp.zeros_like(xnew)
    rs[...] = jnp.zeros_like(rs)
    loads[6].wait()
    wide[0 : 2 * tokens, :] = cot_v[...].astype(F32)
    for p in range(2):
        xc[:, feats + p * 128 : feats + (p + 1) * 128] = wide[pl.ds(p, tokens, stride=2), :].astype(BF)
    loads[7].wait()
    loads[8].wait()

    pl.semaphore_wait(barrier, len(peers))

    def spread_rows(stage, rows):
        for dp in near:
            send(stage, rows, rows, dp, t)

    send(1, ga.at[0, s], ga.at[1, s], partner, t)
    spread_rows(0, ga.at[0, s])
    send(17, pack.at[0], pack.at[1], partner, t)
    half_rows = dec_v.shape[0] // 2

    def send_decode(first, count):
        these = pl.ds(first, count)
        send(18, dec2.at[0, these], dec2.at[1, these], partner, t)


    def project(half):
        wide[0 : group * 16, :] = ga[half].reshape(group * 16, 128).astype(F32)
        for p in range(2):
            for c in range(6):
                piece = wide[pl.ds(p * 6 + c, group, stride=16), :].astype(BF)
                if c < 5:
                    fac[half, p * group : (p + 1) * group, c * 128 : (c + 1) * 128] = piece
                else:
                    rows = slice((2 + p) * group, (3 + p) * group)
                    fac[half, rows, feats + p * 128 : feats + (p + 1) * 128] = piece
        lbf[half] = dot(xc[...], fac[half], 1, 1)
        lbs[half] = lbf[half].astype(BF).reshape(lbs.shape[1:])
        for k, tt in quad:
            send(3 + half, lbs.at[half, lax.rem(tt, quads)], l1.at[half, k - 1], me, tt)

    part = tokens // quads

    def sum_quad(half):
        if quads > 1:
            arrive(3 + half, l1.at[half])
        total = lbf[half, pl.ds(pl.multiple_of(ti * part, part), part), :]
        for k in range(quads - 1):
            total = total + l1[half, k].astype(F32)
        lbf[half, 0:part, :] = total
        l2s[half] = total.astype(BF)
        send(5 + half, l2s.at[half], l2.at[half], me, opposite)

    def sum_all(half):
        arrive(5 + half, l2.at[half])
        lfull[half, ti] = (lbf[half, 0:part, :] + l2[half].astype(F32)).astype(BF)
        for k, tt in quad:
            send(7 + half, lfull.at[half, ti], lfull.at[half, ti], me, tt)

    def gradients(half):
        if quads > 1:
            arrive(7 + half, lfull.at[half, pl.ds(0, quads - 1)])
        if half == 1:
            send_decode(half_rows, half_rows)
        both = lfull[half].reshape(tokens, 4 * group)
        g = adapter_scale_factor * dot(both, xc[...], 0, 0)
        for p in range(2):
            for c in range(5):
                gr[half, pl.ds(p * 6 + c, group, stride=12), :] = g[
                    (2 + p) * group : (3 + p) * group, c * 128 : (c + 1) * 128
                ]
            gr[half, pl.ds(p * 6 + 5, group, stride=12), :] = g[
                p * group : (p + 1) * group, feats + p * 128 : feats + (p + 1) * 128
            ]
        for k, pp in plane:
            src = gr.at[half, pl.ds(pl.multiple_of(pp * 24, 24), 24)]
            send(9 + half, src, r1.at[half, k - 1], device(pp, zh, co), t)

    def sum_plane(half):
        if planes > 1:
            arrive(9 + half, r1.at[half])
        total = gr[half, pl.ds(pl.multiple_of(xy * 24, 24), 24), :]
        for k in range(planes - 1):
            total = total + r1[half, k]
        for c in range(2):
            rs[half, c, :12, :] = total[c * 12 : (c + 1) * 12, :]
        send(11 + half, rs.at[half, other_co], r2.at[half, 0], device(xy, zh, other_co), t)
        send(14 - half, rs.at[half, co], r2.at[1 - half, 1], partner, t)
        send(14 - half, rs.at[half, other_co], r2.at[1 - half, 2], cross, t)

    arrive(0, ga.at[0, pl.ds(0, group - 1)])
    send_decode(0, half_rows)
    project(0)
    arrive(1, ga.at[1, s])
    spread_rows(2, ga.at[1, s])
    sum_quad(0)
    arrive(2, ga.at[1, pl.ds(0, group - 1)])
    project(1)
    sum_all(0)
    sum_quad(1)
    gradients(0)
    sum_all(1)
    sum_plane(0)
    gradients(1)
    loads[9].wait()
    loads[10].wait()
    for p in range(2):
        base[:, p * 128 : (p + 1) * 128] = dot(dec_v[...], frz_v[p], 1, 0)

    sum_plane(1)

    def update(half):
        arrive(11 + half, r2.at[half, 0])
        arrive(13 + half, r2.at[half, pl.ds(1, 2)])
        grad = (rs[half, co] + r2[half, 0]) + (r2[half, 1] + r2[half, 2])
        return adam_step(pack[half, 0], pack[half, 1], pack[half, 2], grad)

    def unpack_new(half, pieces):
        wide[0 : group * 16, :] = gb[half].reshape(group * 16, 128).astype(F32)
        for p in range(2):
            for c in pieces:
                piece = wide[pl.ds(p * 6 + c, group, stride=16), :].astype(BF)
                if c < 5:
                    enew[p * group : (p + 1) * group, c * 128 : (c + 1) * 128] = piece
                else:
                    rows = slice((half * 2 + p) * group, (half * 2 + p + 1) * group)
                    xnew[rows, p * 128 : (p + 1) * 128] = piece

    arrive(17, pack.at[1])
    gb[1, s] = update(1)[0].astype(BF)
    spread_rows(15, gb.at[1, s])
    arrive(18, dec2.at[1])
    arrive(15, gb.at[1, pl.ds(0, group - 1)])
    unpack_new(1, range(5))
    inner = []
    for i in (1, 0):
        v = adapter_scale_factor * dot(dec2[i], enew[...], 1, 1)
        inner.append(jnp.concatenate([v[:half_rows], v[half_rows:]], axis=1))
        zs[1 - i] = inner[-1].astype(BF)
        if i == 1:
            for k in far:
                send(20, zs.at[0], zx.at[k], partner, lax.rem(t + k, nt))
    for k, tt in tens:
        send(16, zs.at[1], zl.at[k - 1], me, tt)
    unpack_new(1, (5,))

    after, moment, square = update(0)
    gb[0, s] = after.astype(BF)
    spread_rows(19, gb.at[0, s])
    for i, value in enumerate((after, moment, square)):
        new_o[i] = value
    arrive(19, gb.at[0, pl.ds(0, group - 1)])
    unpack_new(0, (5,))

    arrive(16, zl)
    arrive(20, zx)
    own, other = zx[0].astype(F32), inner[1]
    for k in range(nt - 1):
        own = own + zx[k + 1].astype(F32)
        other = other + zl[k].astype(F32)
    both = jnp.concatenate(
        [
            jnp.concatenate([v[:, : 2 * group], v[:, 2 * group :]], axis=0)
            for v in (own.astype(BF), other.astype(BF))
        ],
        axis=1,
    )
    out = base[...] + dot(both, xnew[...], 1, 0)
    rows = 2 * half_rows
    for p in range(2):
        wide[pl.ds(p, rows, stride=2), :] = out[:, p * 128 : (p + 1) * 128]
    proj_o[...] = wide[0 : 2 * rows, :].astype(BF)

    for stage, ref in sent:
        descriptor(stage, ref).wait_send()


def spread(new, proj, *rest):
    outs, parts, sem = rest[:7], rest[7:13], rest[13]
    copies = [pltpu.make_async_copy(proj, outs[0], sem.at[0])]
    copies[0].start()
    for i, (e, o) in enumerate(((0, 1), (2, 4), (3, 5))):
        for p in range(2):
            for c in range(5):
                row = p * 6 + c
                parts[e][p, :, c * 128 : (c + 1) * 128] = new[i, row : row + 1, :]
            parts[o][p, :, :] = new[i, p * 6 + 5 : p * 6 + 6, :]
        for n in (e, o):
            copies.append(pltpu.make_async_copy(parts[n], outs[n + 1], sem.at[n + 1]))
            copies[-1].start()
    for copy in copies:
        copy.wait()


def body(nx, ny, nt, x, cot, frz, dec, em, xm, emo, esq, xmo, xsq):
    tokens, feats = x.shape
    rows = dec.shape[0]
    planes = nx * ny
    group = planes * 2
    quads = nt // 2
    part = tokens // quads
    hbm = pl.BlockSpec(memory_space=pltpu.HBM)
    vmem = pl.BlockSpec(memory_space=pltpu.VMEM)
    like = lambda a: jax.ShapeDtypeStruct(a.shape, a.dtype)
    held = lambda a: pltpu.VMEM(a.shape, a.dtype)
    proj, new = pl.pallas_call(
        functools.partial(kernel, nx, ny, nt),
        out_shape=(
            jax.ShapeDtypeStruct((rows * 2, 128), BF),
            jax.ShapeDtypeStruct((3, 16, 128), F32),
        ),
        in_specs=[hbm] * 10,
        out_specs=[vmem] * 2,
        scratch_shapes=[
            held(em), held(xm), held(em), held(xm), held(em), held(xm),
            pltpu.VMEM((tokens, feats + 256), BF),
            pltpu.VMEM((tokens * 2, 128), BF),
            held(frz),
            held(dec),
            pltpu.VMEM((2, rows, feats), BF),
            pltpu.VMEM((max(2 * tokens, group * 16) + 16, 128), F32),
            pltpu.VMEM((rows, 256), F32),
            pltpu.VMEM((2, 3, 16, 128), F32),
            pltpu.VMEM((2, group, 16, 128), BF),
            pltpu.VMEM((2, group, 16, 128), BF),
            pltpu.VMEM((2, 4 * group, feats + 256), BF),
            pltpu.VMEM((2 * group, feats), BF),
            pltpu.VMEM((4 * group, 256), BF),
            pltpu.VMEM((2, tokens, 4 * group), F32),
            pltpu.VMEM((2, quads, part, 4 * group), BF),
            pltpu.VMEM((2, max(quads - 1, 1), part, 4 * group), BF),
            pltpu.VMEM((2, part, 4 * group), BF),
            pltpu.VMEM((2, part, 4 * group), BF),
            pltpu.VMEM((2, quads, part, 4 * group), BF),
            pltpu.VMEM((2, group * 12 + 16, 128), F32),
            pltpu.VMEM((2, max(planes - 1, 1), 24, 128), F32),
            pltpu.VMEM((2, 2, 16, 128), F32),
            pltpu.VMEM((2, 3, 16, 128), F32),
            pltpu.VMEM((2, rows // 2, 4 * group), BF),
            pltpu.VMEM((nt - 1, rows // 2, 4 * group), BF),
            pltpu.VMEM((nt, rows // 2, 4 * group), BF),
            pltpu.SemaphoreType.DMA((11,)),
            pltpu.SemaphoreType.DMA((21,)),
            pltpu.SemaphoreType.DMA((21,)),
        ],
        compiler_params=pltpu.CompilerParams(
            collective_id=0, has_side_effects=True, vmem_limit_bytes=63 * 1024 * 1024
        ),
        cost_estimate=pl.CostEstimate(flops=600_000_000, bytes_accessed=5_000_000, transcendentals=0),
    )(x, cot.reshape(tokens * 2, 128), frz, dec, em, xm, emo, esq, xmo, xsq)
    factors = [em, xm, em, em, xm, xm]
    out = pl.pallas_call(
        spread,
        out_shape=(like(proj),) + tuple(like(f) for f in factors),
        in_specs=[vmem] * 2,
        out_specs=[hbm] * 7,
        scratch_shapes=[held(f) for f in factors] + [pltpu.SemaphoreType.DMA((7,))],
        cost_estimate=pl.CostEstimate(flops=10_000, bytes_accessed=60_000, transcendentals=0),
    )(new, proj)
    return (out[0].reshape(rows, 2, 128),) + tuple(out[1:])


def solution(mesh):
    nt = mesh.shape["tensor"]
    planes = mesh.shape["dp"] // QUAD
    ny = min(planes, 4)
    nx = planes // ny
    factor = P(None, "dp", "tensor")
    return jax.shard_map(
        functools.partial(body, nx, ny, nt),
        mesh=mesh,
        in_specs=(
            P("dp", "tensor"),
            P("dp", None, "tensor"),
            P(None, None, "tensor"),
            P("dp", None),
        )
        + (factor,) * 6,
        out_specs=(P("dp", None, "tensor"),) + (factor,) * 6,
        check_vma=False,
    )
```
